32 devices in a mesh: dp: 16 (over z, y, x), chan: 2 (over core).
Axes of the slice: x: 2, y: 2, z: 4, core: 2. Of those that a mesh axis runs over, the one named last changes fastest.
Arguments:
- boards: bfloat16 [32, 19, 19, 256], P('dp', None, None, 'chan'), may hold values from -110 to 110
- weights: bfloat16 [6, 9, 256, 256], P(None, None, None, 'chan'), may hold values from -0.125 to 0.125
- gains: float32 [6, 256], P(None, 'chan'), may hold values from 0.5 to 1.5
- shifts: float32 [6, 256], P(None, 'chan'), may hold values from -3 to 3
Outputs:
- features: bfloat16 [32, 19, 19, 256], P('dp', None, None, 'chan')
The draws below stay inside these ranges and needn't reach their ends.
All inputs are finite; a program needn't handle non-finite values.
Results may differ from the reference program's by a relative error of at most 0.0065.
Values may be sent and summed in bfloat16 or wider, within the bound.
A program may use at most 64 MiB of HBM per device.

```python
import math
import jax
import jax.numpy as jnp
from jax import lax

CH = 256
SIDE = 19
LAYERS = 6
BOARDS = 32


def draw_boards(key, part):
    key_scale = jax.random.fold_in(key, 11)
    key_value = jax.random.fold_in(key, 12)
    key_common = jax.random.fold_in(key, 13)
    position = jnp.arange(BOARDS, dtype=jnp.float32) / max(BOARDS - 1, 1)
    rising = 1.0 + 9.0 * position
    spread = jnp.exp(jax.random.uniform(key_scale, (BOARDS,), jnp.float32, 0.0, math.log(2.0)))
    scale = (rising * spread).reshape(BOARDS, 1, 1, 1)
    values = jnp.clip(jax.random.normal(key_value, (BOARDS, SIDE, SIDE, CH), jnp.float32), -3.5, 3.5)
    common = jnp.clip(jax.random.normal(key_common, (1, 1, 1, CH), jnp.float32), -2.0, 2.0)
    values = values + 0.7 * common
    return (values * scale).astype(jnp.bfloat16)


def levels(key, extent, shards, low, top_value):
    loudness, own = 1.0, jax.random.fold_in(key, 6)
    for dim, parts in shards:
        draws = jnp.exp(jax.random.uniform(jax.random.fold_in(own, dim), (parts,), jnp.float32, low / len(shards), top_value / len(shards)))
        loudness = loudness * jnp.repeat(draws, extent[dim] // parts).reshape([-1 if axis == dim else 1 for axis in range(len(extent))])
    return loudness


def bell_draw(own_key, shape, scale, limit, pieces=(), kind=jnp.bfloat16):
    gain = levels(own_key, shape, pieces, -0.22, 0.18) if pieces else 1.0
    entries = jax.random.normal(own_key, shape, jnp.float32) * scale * gain
    return jnp.minimum(jnp.maximum(entries, -limit), limit).astype(kind)


def setup_inputs(seed: int = 0) -> dict:
    arg_keys = jax.random.split(jax.random.key(seed), 5)
    return {
        "boards": draw_boards(jax.random.fold_in(arg_keys[4], 71), 0),
        "weights": bell_draw(arg_keys[1], (LAYERS, 9, CH, CH), (9 * CH) ** -0.5, 0.125, ((3, 2),)),
        "gains": jnp.clip(1.0 + 0.1 * jax.random.normal(arg_keys[2], (LAYERS, CH), jnp.float32), 0.5, 1.5),
        "shifts": bell_draw(arg_keys[3], (LAYERS, CH), 0.5, 3.0, ((1, 2),), jnp.float32),
    }


EPSILON = 1e-05

def conv_taps(inputs, kernel):
    side = inputs.shape[1]
    padded = jnp.pad(inputs, ((0, 0), (1, 1), (1, 1), (0, 0)))
    total = jnp.zeros((inputs.shape[0] * side * side, kernel.shape[2]), jnp.float32)
    for tap in range(9):
        row, col = divmod(tap, 3)
        window = padded[:, row:row + side, col:col + side, :].reshape(-1, inputs.shape[3])
        total = total + jnp.dot(window, kernel[tap], preferred_element_type=jnp.float32)
    return total.reshape(inputs.shape[0], side, side, kernel.shape[2])

def reference(boards, weights, gains, shifts):
    current = boards
    skipped = boards
    for layer in range(LAYERS):
        if layer % 2 == 0:
            skipped = current
        out = conv_taps(current, weights[layer])
        mean = lax.optimization_barrier(jnp.mean(out, axis=(0, 1, 2)))
        var = lax.optimization_barrier(jnp.mean((out - mean) ** 2, axis=(0, 1, 2)))
        normed = (out - mean) * lax.rsqrt(var + EPSILON) * gains[layer] + shifts[layer]
        if layer % 2 == 1:
            normed = normed + skipped.astype(jnp.float32)
        current = jnp.maximum(normed, 0.0).astype(jnp.bfloat16)
    return current
```

```python
import functools

import jax
import jax.numpy as jnp
from jax import lax
from jax.experimental import pallas as pl
from jax.experimental.pallas import tpu as pltpu
from jax.sharding import PartitionSpec as P

EPSILON = 1e-05
MESH = pl.DeviceIdType.MESH
LANES = 128


def round_up(value, step):
    return -(-value // step) * step


def stack_kernel(
    ndp, nch, side, mine, layers, rows, base,
    boards, weights, gains, shifts, out,
    board_own, board_other, wbuf, aff, xf, skip, mask, lhs, zbuf, stats, stage,
    own_sem, x_send, x_recv, w_local, w_send, w_recv, s_send, s_recv, o_send, o_recv,
):
    dp = lax.axis_index("dp")
    me = lax.axis_index("chan")
    other = 1 - me
    partner = (dp, other)
    total = ndp * nch
    flat_me = dp * nch + me
    stride = side + 1
    points = mine * side * side

    def peer(step):
        flat = lax.rem(flat_me + step, total)
        return (lax.div(flat, nch), lax.rem(flat, nch))

    def every_peer(body):
        if total <= 64:
            for step in range(1, total):
                body(step)
        else:
            def one(step, carry):
                body(step)
                return carry
            lax.fori_loop(1, total, one, 0)

    barrier = pltpu.get_barrier_semaphore()
    every_peer(lambda step: pl.semaphore_signal(barrier, inc=1, device_id=peer(step), device_id_type=MESH))

    own = pltpu.make_async_copy(boards.at[pl.ds(me * mine, mine)], board_own, own_sem)
    own.start()

    def weight_local(layer):
        return pltpu.make_async_copy(weights.at[layer], wbuf.at[me, layer], w_local.at[layer])

    def weight_remote(layer, half):
        return pltpu.make_async_remote_copy(
            src_ref=weights.at[layer], dst_ref=wbuf.at[half, layer],
            send_sem=w_send.at[layer], recv_sem=w_recv.at[layer],
            device_id=partner, device_id_type=MESH,
        )

    def swap(index, src, dst):
        return pltpu.make_async_remote_copy(
            src_ref=src, dst_ref=dst, send_sem=x_send.at[index], recv_sem=x_recv.at[index],
            device_id=partner, device_id_type=MESH,
        )

    for layer in range(layers):
        weight_local(layer).start()
    xf[...] = jnp.zeros_like(xf)
    mask[...] = jnp.zeros_like(mask)
    for n in range(mine):
        for i in range(side):
            mask[pl.ds((n * stride + i) * stride, side), :] = jnp.ones((side, LANES), jnp.float32)
    aff[me, 0] = gains[...]
    aff[me, 1] = shifts[...]

    pl.semaphore_wait(barrier, total - 1)
    swaps = [
        swap(0, boards.at[pl.ds(other * mine, mine)], board_other),
        swap(1, gains, aff.at[me, 0]),
        swap(2, shifts, aff.at[me, 1]),
    ]
    swaps[0].start()
    weight_remote(0, me).start()
    swaps[1].start()
    swaps[2].start()
    for layer in range(1, layers):
        weight_remote(layer, me).start()

    def place(half, source):
        for n in range(mine):
            for i in range(side):
                at = base + (n * stride + i) * stride
                xf[half, pl.ds(at, side), :] = source[n, i].astype(jnp.float32)

    own.wait()
    place(me, board_own)
    swaps[0].wait_recv()
    place(other, board_other)
    swaps[1].wait_recv()
    swaps[2].wait_recv()

    def layer_step(layer, carry):
        odd = lax.rem(layer, 2)

        @pl.when(odd == 0)
        def _():
            for half in range(nch):
                skip[half] = xf[half, pl.ds(base, rows), :]

        for tap in range(9):
            a, b = divmod(tap, 3)
            at = base + (a - 1) * stride + (b - 1)
            for half in range(nch):
                column = (tap * nch + half) * LANES
                lhs[:, pl.ds(column, LANES)] = xf[half, pl.ds(at, rows), :].astype(jnp.bfloat16)
        weight_local(layer).wait()
        weight_remote(layer, other).wait_recv()
        kernel = jnp.concatenate([wbuf[half, layer] for half in range(nch)], axis=1)
        zbuf[...] = jnp.dot(lhs[...], kernel, preferred_element_type=jnp.float32)

        centre = (side // 2) * stride + side // 2
        for half in range(nch):
            lanes = pl.ds(half * LANES, LANES)
            middle = zbuf[pl.ds(centre, 1), lanes]
            away = (zbuf[:, lanes] - middle) * mask[...]
            first = jnp.sum(away, axis=0, keepdims=True)
            second = jnp.sum(away * away, axis=0, keepdims=True)
            stats[layer, flat_me, pl.ds(half, 1), :] = middle + first * (1.0 / points)
            stats[layer, flat_me, pl.ds(nch + half, 1), :] = second - first * first * (1.0 / points)

        def send(step):
            pltpu.make_async_remote_copy(
                src_ref=stats.at[layer, flat_me], dst_ref=stats.at[layer, flat_me],
                send_sem=s_send.at[layer], recv_sem=s_recv.at[layer],
                device_id=peer(step), device_id_type=MESH,
            ).start()

        every_peer(send)
        arrived = stats.at[layer, pl.ds(0, total - 1)]
        pltpu.make_async_copy(arrived, arrived, s_recv.at[layer]).wait()

        seen = stats[layer]
        mean = jnp.sum(seen, axis=0)[:nch] * (1.0 / total)
        drift = seen[:, :nch] - mean[None]
        var = (jnp.sum(seen[:, nch:], axis=0) + points * jnp.sum(drift * drift, axis=0)) * (1.0 / (points * total))
        inverse = lax.rsqrt(var + EPSILON)
        keep = odd.astype(jnp.float32)
        for half in range(nch):
            gain = aff[half, 0, pl.ds(layer, 1), :] * inverse[half : half + 1]
            shift = aff[half, 1, pl.ds(layer, 1), :]
            normed = (zbuf[:, pl.ds(half * LANES, LANES)] - mean[half : half + 1]) * gain + shift
            normed = normed + skip[half] * keep
            fresh = jnp.maximum(normed, 0.0) * mask[...]
            xf[half, pl.ds(base, rows), :] = fresh.astype(jnp.bfloat16).astype(jnp.float32)
        return carry

    lax.fori_loop(0, layers, layer_step, 0)

    def collect(half, target, first):
        for n in range(mine):
            for i in range(side):
                at = base + (n * stride + i) * stride
                target[first + n, i] = xf[half, pl.ds(at, side), :].astype(jnp.bfloat16)

    collect(other, stage, 0)
    final = pltpu.make_async_remote_copy(
        src_ref=stage, dst_ref=out.at[pl.ds(me * mine, mine)],
        send_sem=o_send, recv_sem=o_recv, device_id=partner, device_id_type=MESH,
    )
    final.start()
    collect(me, out, me * mine)

    for one in swaps:
        one.wait_send()

    def drain(layer, carry):
        weight_remote(layer, me).wait_send()
        sent = stats.at[layer, pl.ds(0, total - 1)]
        pltpu.make_async_copy(sent, sent, s_send.at[layer]).wait()
        return carry

    lax.fori_loop(0, layers, drain, 0)
    final.wait()


def on_device(ndp, nch, boards, weights, gains, shifts):
    held, side, _, width = boards.shape
    layers = weights.shape[0]
    mine = held // nch
    stride = side + 1
    rows = round_up((mine - 1) * stride * stride + side * stride, 16)
    base = round_up(stride + 1, 8)
    span = round_up(base + rows + stride + 1, 8)
    total = ndp * nch
    depth = 9 * width * nch
    dma = pltpu.SemaphoreType.DMA
    any_space = pl.BlockSpec(memory_space=pl.ANY)
    vmem = pl.BlockSpec(memory_space=pltpu.VMEM)
    return pl.pallas_call(
        functools.partial(stack_kernel, ndp, nch, side, mine, layers, rows, base),
        out_shape=jax.ShapeDtypeStruct(boards.shape, jnp.bfloat16),
        in_specs=[any_space, any_space, vmem, vmem],
        out_specs=vmem,
        scratch_shapes=[
            pltpu.VMEM((mine, side, side, width), jnp.bfloat16),
            pltpu.VMEM((mine, side, side, width), jnp.bfloat16),
            pltpu.VMEM((nch, layers, depth, width), jnp.bfloat16),
            pltpu.VMEM((nch, 2, layers, width), jnp.float32),
            pltpu.VMEM((nch, span, width), jnp.float32),
            pltpu.VMEM((nch, rows, width), jnp.float32),
            pltpu.VMEM((rows, width), jnp.float32),
            pltpu.VMEM((rows, depth), jnp.bfloat16),
            pltpu.VMEM((rows, width * nch), jnp.float32),
            pltpu.VMEM((layers, total, 2 * nch, width), jnp.float32),
            pltpu.VMEM((mine, side, side, width), jnp.bfloat16),
            dma, dma((3,)), dma((3,)),
            dma((layers,)), dma((layers,)), dma((layers,)),
            dma((layers,)), dma((layers,)), dma, dma,
        ],
        compiler_params=pltpu.CompilerParams(
            collective_id=0, has_side_effects=True, vmem_limit_bytes=40 * 1024 * 1024
        ),
        cost_estimate=pl.CostEstimate(
            flops=2 * layers * rows * depth * width * nch,
            bytes_accessed=2 * weights.size + 4 * boards.size,
            transcendentals=0,
        ),
    )(boards, weights.reshape(layers, depth, width), gains, shifts)


def solution(mesh):
    placed = (
        P("dp", None, None, "chan"),
        P(None, None, None, "chan"),
        P(None, "chan"),
        P(None, "chan"),
    )
    return jax.shard_map(
        functools.partial(on_device, mesh.shape["dp"], mesh.shape["chan"]),
        mesh=mesh,
        in_specs=placed,
        out_specs=P("dp", None, None, "chan"),
        check_vma=False,
    )
```

```python
import functools

import jax
import jax.numpy as jnp
from jax import lax
from jax.experimental import pallas as pl
from jax.experimental.pallas import tpu as pltpu
from jax.sharding import PartitionSpec as P

EPSILON = 1e-05
MESH = pl.DeviceIdType.MESH
LANES = 128


def round_up(value, step):
    return -(-value // step) * step


def stack_kernel(
    ndp, nch, inner, side, mine, layers, rows, base,
    boards, weights, gains, shifts, out,
    board_own, board_other, wbuf, aff, xf, skip, mask, lhs, zbuf, near, far, stage,
    own_sem, x_send, x_recv, w_local, w_send, w_recv, n_send, n_recv, f_send, f_recv, o_send, o_recv,
):
    dp = lax.axis_index("dp")
    me = lax.axis_index("chan")
    other = 1 - me
    partner = (dp, other)
    total = ndp * nch
    stride = side + 1
    points = mine * side * side

    outer = ndp // inner
    group = inner * nch
    plane, spot = lax.div(dp, inner), lax.rem(dp, inner)
    near_me = spot * nch + me

    def near_peer(step):
        flat = lax.rem(near_me + step, group)
        return (plane * inner + lax.div(flat, nch), lax.rem(flat, nch))

    def far_peer(step):
        return (lax.rem(plane + step, outer) * inner + spot, me)

    barrier = pltpu.get_barrier_semaphore()
    for count, peer in ((group, near_peer), (outer, far_peer)):
        for step in range(1, count):
            pl.semaphore_signal(barrier, inc=1, device_id=peer(step), device_id_type=MESH)

    own = pltpu.make_async_copy(boards.at[pl.ds(me * mine, mine)], board_own, own_sem)
    own.start()

    def weight_local(layer):
        return pltpu.make_async_copy(weights.at[layer], wbuf.at[me, layer], w_local.at[layer])

    def weight_remote(layer, half):
        return pltpu.make_async_remote_copy(
            src_ref=weights.at[layer], dst_ref=wbuf.at[half, layer],
            send_sem=w_send.at[layer], recv_sem=w_recv.at[layer],
            device_id=partner, device_id_type=MESH,
        )

    def swap(index, src, dst):
        return pltpu.make_async_remote_copy(
            src_ref=src, dst_ref=dst, send_sem=x_send.at[index], recv_sem=x_recv.at[index],
            device_id=partner, device_id_type=MESH,
        )

    for layer in range(layers):
        weight_local(layer).start()
    xf[...] = jnp.zeros_like(xf)
    mask[...] = jnp.zeros_like(mask)
    for n in range(mine):
        for i in range(side):
            mask[pl.ds((n * stride + i) * stride, side), :] = jnp.ones((side, LANES), jnp.float32)
    aff[me, 0] = gains[...]
    aff[me, 1] = shifts[...]

    pl.semaphore_wait(barrier, group - 1 + outer - 1)
    swaps = [
        swap(0, boards.at[pl.ds(other * mine, mine)], board_other),
        swap(1, gains, aff.at[me, 0]),
        swap(2, shifts, aff.at[me, 1]),
    ]
    swaps[0].start()
    weight_remote(0, me).start()
    swaps[1].start()
    swaps[2].start()
    for layer in range(1, layers):
        weight_remote(layer, me).start()

    def place(half, source):
        for n in range(mine):
            for i in range(side):
                at = base + (n * stride + i) * stride
                xf[half, pl.ds(at, side), :] = source[n, i].astype(jnp.float32)

    own.wait()
    place(me, board_own)
    swaps[0].wait_recv()
    place(other, board_other)
    swaps[1].wait_recv()
    swaps[2].wait_recv()

    def exchange(slots, layer, place_me, count, peer, send_sem, recv_sem):
        for step in range(1, count):
            pltpu.make_async_remote_copy(
                src_ref=slots.at[layer, place_me], dst_ref=slots.at[layer, place_me],
                send_sem=send_sem.at[layer], recv_sem=recv_sem.at[layer],
                device_id=peer(step), device_id_type=MESH,
            ).start()
        await_slots(slots, layer, count, recv_sem)

    def await_slots(slots, layer, count, sem):
        those = slots.at[layer, pl.ds(0, count - 1)]
        pltpu.make_async_copy(those, those, sem.at[layer]).wait()

    def merge(seen, each):
        mean = jnp.sum(seen[:, :nch], axis=0) * (1.0 / seen.shape[0])
        drift = seen[:, :nch] - mean[None]
        spread = jnp.sum(seen[:, nch:], axis=0) + each * jnp.sum(drift * drift, axis=0)
        return mean, spread

    def layer_step(layer, carry):
        odd = lax.rem(layer, 2)

        @pl.when(odd == 0)
        def _():
            for half in range(nch):
                skip[half] = xf[half, pl.ds(base, rows), :]

        for tap in range(9):
            a, b = divmod(tap, 3)
            at = base + (a - 1) * stride + (b - 1)
            for half in range(nch):
                column = (tap * nch + half) * LANES
                lhs[:, pl.ds(column, LANES)] = xf[half, pl.ds(at, rows), :].astype(jnp.bfloat16)
        weight_local(layer).wait()
        weight_remote(layer, other).wait_recv()
        kernel = jnp.concatenate([wbuf[half, layer] for half in range(nch)], axis=1)
        zbuf[...] = jnp.dot(lhs[...], kernel, preferred_element_type=jnp.float32)

        centre = (side // 2) * stride + side // 2
        for half in range(nch):
            lanes = pl.ds(half * LANES, LANES)
            middle = zbuf[pl.ds(centre, 1), lanes]
            away = (zbuf[:, lanes] - middle) * mask[...]
            first = jnp.sum(away, axis=0, keepdims=True)
            second = jnp.sum(away * away, axis=0, keepdims=True)
            near[layer, near_me, pl.ds(half, 1), :] = middle + first * (1.0 / points)
            near[layer, near_me, pl.ds(nch + half, 1), :] = second - first * first * (1.0 / points)

        exchange(near, layer, near_me, group, near_peer, n_send, n_recv)
        mean, spread = merge(near[layer], points)
        far[layer, plane, pl.ds(0, nch), :] = mean
        far[layer, plane, pl.ds(nch, nch), :] = spread
        exchange(far, layer, plane, outer, far_peer, f_send, f_recv)
        mean, spread = merge(far[layer], points * group)
        var = spread * (1.0 / (points * total))
        inverse = lax.rsqrt(var + EPSILON)
        keep = odd.astype(jnp.float32)
        for half in range(nch):
            gain = aff[half, 0, pl.ds(layer, 1), :] * inverse[half : half + 1]
            shift = aff[half, 1, pl.ds(layer, 1), :]
            normed = (zbuf[:, pl.ds(half * LANES, LANES)] - mean[half : half + 1]) * gain + shift
            normed = normed + skip[half] * keep
            fresh = jnp.maximum(normed, 0.0) * mask[...]
            xf[half, pl.ds(base, rows), :] = fresh.astype(jnp.bfloat16).astype(jnp.float32)
        return carry

    lax.fori_loop(0, layers, layer_step, 0)

    def collect(half, target, first):
        for n in range(mine):
            for i in range(side):
                at = base + (n * stride + i) * stride
                target[first + n, i] = xf[half, pl.ds(at, side), :].astype(jnp.bfloat16)

    collect(other, stage, 0)
    final = pltpu.make_async_remote_copy(
        src_ref=stage, dst_ref=out.at[pl.ds(me * mine, mine)],
        send_sem=o_send, recv_sem=o_recv, device_id=partner, device_id_type=MESH,
    )
    final.start()
    collect(me, out, me * mine)

    for one in swaps:
        one.wait_send()

    def drain(layer, carry):
        weight_remote(layer, me).wait_send()
        await_slots(near, layer, group, n_send)
        await_slots(far, layer, outer, f_send)
        return carry

    lax.fori_loop(0, layers, drain, 0)
    final.wait()


def on_device(ndp, nch, boards, weights, gains, shifts):
    held, side, _, width = boards.shape
    layers = weights.shape[0]
    mine = held // nch
    stride = side + 1
    rows = round_up((mine - 1) * stride * stride + side * stride, 16)
    base = round_up(stride + 1, 8)
    span = round_up(base + rows + stride + 1, 8)
    inner = 1 << ((ndp.bit_length() - 1) // 2)
    depth = 9 * width * nch
    dma = pltpu.SemaphoreType.DMA
    in_hbm = pl.BlockSpec(memory_space=pltpu.HBM)
    vmem = pl.BlockSpec(memory_space=pltpu.VMEM)
    return pl.pallas_call(
        functools.partial(stack_kernel, ndp, nch, inner, side, mine, layers, rows, base),
        out_shape=jax.ShapeDtypeStruct(boards.shape, jnp.bfloat16),
        in_specs=[in_hbm, in_hbm, vmem, vmem],
        out_specs=vmem,
        scratch_shapes=[
            pltpu.VMEM((mine, side, side, width), jnp.bfloat16),
            pltpu.VMEM((mine, side, side, width), jnp.bfloat16),
            pltpu.VMEM((nch, layers, depth, width), jnp.bfloat16),
            pltpu.VMEM((nch, 2, layers, width), jnp.float32),
            pltpu.VMEM((nch, span, width), jnp.float32),
            pltpu.VMEM((nch, rows, width), jnp.float32),
            pltpu.VMEM((rows, width), jnp.float32),
            pltpu.VMEM((rows, depth), jnp.bfloat16),
            pltpu.VMEM((rows, width * nch), jnp.float32),
            pltpu.VMEM((layers, inner * nch, 2 * nch, width), jnp.float32),
            pltpu.VMEM((layers, ndp // inner, 2 * nch, width), jnp.float32),
            pltpu.VMEM((mine, side, side, width), jnp.bfloat16),
            dma, dma((3,)), dma((3,)),
            dma((layers,)), dma((layers,)), dma((layers,)),
            dma((layers,)), dma((layers,)), dma((layers,)), dma((layers,)), dma, dma,
        ],
        compiler_params=pltpu.CompilerParams(
            collective_id=0, has_side_effects=True, vmem_limit_bytes=62 * 1024 * 1024
        ),
        cost_estimate=pl.CostEstimate(
            flops=2 * layers * rows * depth * width * nch,
            bytes_accessed=2 * weights.size + 4 * boards.size,
            transcendentals=0,
        ),
    )(boards, weights.reshape(layers, depth, width), gains, shifts)


def solution(mesh):
    placed = (
        P("dp", None, None, "chan"),
        P(None, None, None, "chan"),
        P(None, "chan"),
        P(None, "chan"),
    )
    return jax.shard_map(
        functools.partial(on_device, mesh.shape["dp"], mesh.shape["chan"]),
        mesh=mesh,
        in_specs=placed,
        out_specs=P("dp", None, None, "chan"),
        check_vma=False,
    )
```

```python
import functools

import jax
import jax.numpy as jnp
from jax import lax
from jax.experimental import pallas as pl
from jax.experimental.pallas import tpu as pltpu
from jax.sharding import PartitionSpec as P

EPSILON = 1e-05
MESH = pl.DeviceIdType.MESH
LANES = 128
VMEM_LIMIT = 57 * 1024 * 1024


def round_up(value, step):
    return -(-value // step) * step


def stack_kernel(
    ndp, nch, side, mine, layers, rows, base,
    boards, weights, gains, shifts, out,
    board_own, board_other, wbuf, aff, xf, skip, mask, lhs, zbuf, stats, stage,
    own_sem, a_local, x_send, x_recv, w_local, w_send, w_recv, s_send, s_recv, o_send, o_recv,
):
    dp = lax.axis_index("dp")
    me = lax.axis_index("chan")
    other = 1 - me
    partner = (dp, other)
    total = ndp * nch
    flat_me = dp * nch + me
    stride = side + 1
    points = mine * side * side

    def peer(step):
        flat = lax.rem(flat_me + step, total)
        return (lax.div(flat, nch), lax.rem(flat, nch))

    def every_peer(body):
        if total <= 64:
            for step in range(1, total):
                body(step)
        else:
            def one(step, carry):
                body(step)
                return carry
            lax.fori_loop(1, total, one, 0)

    barrier = pltpu.get_barrier_semaphore()
    every_peer(lambda step: pl.semaphore_signal(barrier, inc=1, device_id=peer(step), device_id_type=MESH))

    own = pltpu.make_async_copy(boards.at[pl.ds(me * mine, mine)], board_own, own_sem)
    own.start()
    affine = [
        pltpu.make_async_copy(gains, aff.at[me, 0], a_local.at[0]),
        pltpu.make_async_copy(shifts, aff.at[me, 1], a_local.at[1]),
    ]
    for one in affine:
        one.start()

    def weight_local(layer):
        return pltpu.make_async_copy(weights.at[layer], wbuf.at[me, layer], w_local.at[layer])

    def weight_remote(layer, half):
        return pltpu.make_async_remote_copy(
            src_ref=weights.at[layer], dst_ref=wbuf.at[half, layer],
            send_sem=w_send.at[layer], recv_sem=w_recv.at[layer],
            device_id=partner, device_id_type=MESH,
        )

    def swap(index, src, dst):
        return pltpu.make_async_remote_copy(
            src_ref=src, dst_ref=dst, send_sem=x_send.at[index], recv_sem=x_recv.at[index],
            device_id=partner, device_id_type=MESH,
        )

    for layer in range(layers):
        weight_local(layer).start()
    xf[...] = jnp.zeros_like(xf)
    mask[...] = jnp.zeros_like(mask)
    for n in range(mine):
        for i in range(side):
            mask[pl.ds((n * stride + i) * stride, side), :] = jnp.ones((side, LANES), jnp.float32)

    pl.semaphore_wait(barrier, total - 1)
    swaps = [
        swap(0, boards.at[pl.ds(other * mine, mine)], board_other),
        swap(1, gains, aff.at[me, 0]),
        swap(2, shifts, aff.at[me, 1]),
    ]
    swaps[0].start()
    weight_remote(0, me).start()
    swaps[1].start()
    swaps[2].start()

    def place(half, source):
        for n in range(mine):
            for i in range(side):
                at = base + (n * stride + i) * stride
                xf[half, pl.ds(at, side), :] = source[n, i].astype(jnp.float32)

    own.wait()
    place(me, board_own)
    swaps[0].wait_recv()
    place(other, board_other)
    swaps[1].wait_recv()
    swaps[2].wait_recv()
    for one in affine:
        one.wait()

    def layer_step(layer, carry):
        odd = lax.rem(layer, 2)

        @pl.when(layer + 1 < layers)
        def _():
            weight_remote(layer + 1, me).start()

        @pl.when(odd == 0)
        def _():
            for half in range(nch):
                skip[half] = xf[half, pl.ds(base, rows), :]

        for tap in range(9):
            a, b = divmod(tap, 3)
            at = base + (a - 1) * stride + (b - 1)
            for half in range(nch):
                column = (tap * nch + half) * LANES
                lhs[:, pl.ds(column, LANES)] = xf[half, pl.ds(at, rows), :].astype(jnp.bfloat16)
        weight_local(layer).wait()
        weight_remote(layer, other).wait_recv()
        kernel = jnp.concatenate([wbuf[half, layer] for half in range(nch)], axis=1)
        zbuf[...] = jnp.dot(lhs[...], kernel, preferred_element_type=jnp.float32)

        centre = (side // 2) * stride + side // 2
        for half in range(nch):
            lanes = pl.ds(half * LANES, LANES)
            middle = zbuf[pl.ds(centre, 1), lanes]
            away = (zbuf[:, lanes] - middle) * mask[...]
            first = jnp.sum(away, axis=0, keepdims=True)
            second = jnp.sum(away * away, axis=0, keepdims=True)
            stats[layer, flat_me, pl.ds(half, 1), :] = middle + first * (1.0 / points)
            stats[layer, flat_me, pl.ds(nch + half, 1), :] = second - first * first * (1.0 / points)

        def send(step):
            pltpu.make_async_remote_copy(
                src_ref=stats.at[layer, flat_me], dst_ref=stats.at[layer, flat_me],
                send_sem=s_send.at[layer], recv_sem=s_recv.at[layer],
                device_id=peer(step), device_id_type=MESH,
            ).start()

        every_peer(send)
        arrived = stats.at[layer, pl.ds(0, total - 1)]
        pltpu.make_async_copy(arrived, arrived, s_recv.at[layer]).wait()

        seen = stats[layer]
        mean = jnp.sum(seen, axis=0)[:nch] * (1.0 / total)
        drift = seen[:, :nch] - mean[None]
        var = (jnp.sum(seen[:, nch:], axis=0) + points * jnp.sum(drift * drift, axis=0)) * (1.0 / (points * total))
        inverse = lax.rsqrt(var + EPSILON)
        keep = odd.astype(jnp.float32)
        for half in range(nch):
            gain = aff[half, 0, pl.ds(layer, 1), :] * inverse[half : half + 1]
            shift = aff[half, 1, pl.ds(layer, 1), :]
            normed = (zbuf[:, pl.ds(half * LANES, LANES)] - mean[half : half + 1]) * gain + shift
            normed = normed + skip[half] * keep
            fresh = jnp.maximum(normed, 0.0) * mask[...]
            xf[half, pl.ds(base, rows), :] = fresh.astype(jnp.bfloat16).astype(jnp.float32)
        return carry

    lax.fori_loop(0, layers, layer_step, 0)

    def collect(half, target, first):
        for n in range(mine):
            for i in range(side):
                at = base + (n * stride + i) * stride
                target[first + n, i] = xf[half, pl.ds(at, side), :].astype(jnp.bfloat16)

    collect(other, stage, 0)
    final = pltpu.make_async_remote_copy(
        src_ref=stage, dst_ref=out.at[pl.ds(me * mine, mine)],
        send_sem=o_send, recv_sem=o_recv, device_id=partner, device_id_type=MESH,
    )
    final.start()
    collect(me, out, me * mine)

    for one in swaps:
        one.wait_send()

    def drain(layer, carry):
        weight_remote(layer, me).wait_send()
        sent = stats.at[layer, pl.ds(0, total - 1)]
        pltpu.make_async_copy(sent, sent, s_send.at[layer]).wait()
        return carry

    lax.fori_loop(0, layers, drain, 0)
    final.wait()


def on_device(ndp, nch, boards, weights, gains, shifts):
    held, side, _, width = boards.shape
    layers = weights.shape[0]
    mine = held // nch
    stride = side + 1
    rows = round_up((mine - 1) * stride * stride + side * stride, 16)
    base = round_up(stride + 1, 8)
    span = round_up(base + rows + stride + 1, 8)
    total = ndp * nch
    depth = 9 * width * nch
    dma = pltpu.SemaphoreType.DMA
    in_hbm = pl.BlockSpec(memory_space=pltpu.HBM)
    vmem = pl.BlockSpec(memory_space=pltpu.VMEM)
    return pl.pallas_call(
        functools.partial(stack_kernel, ndp, nch, side, mine, layers, rows, base),
        out_shape=jax.ShapeDtypeStruct(boards.shape, jnp.bfloat16),
        in_specs=[in_hbm] * 4,
        out_specs=vmem,
        scratch_shapes=[
            pltpu.VMEM((mine, side, side, width), jnp.bfloat16),
            pltpu.VMEM((mine, side, side, width), jnp.bfloat16),
            pltpu.VMEM((nch, layers, depth, width), jnp.bfloat16),
            pltpu.VMEM((nch, 2, layers, width), jnp.float32),
            pltpu.VMEM((nch, span, width), jnp.float32),
            pltpu.VMEM((nch, rows, width), jnp.float32),
            pltpu.VMEM((rows, width), jnp.float32),
            pltpu.VMEM((rows, depth), jnp.bfloat16),
            pltpu.VMEM((rows, width * nch), jnp.float32),
            pltpu.VMEM((layers, total, 2 * nch, width), jnp.float32),
            pltpu.VMEM((mine, side, side, width), jnp.bfloat16),
            dma, dma((2,)), dma((3,)), dma((3,)),
            dma((layers,)), dma((layers,)), dma((layers,)),
            dma((layers,)), dma((layers,)), dma, dma,
        ],
        compiler_params=pltpu.CompilerParams(
            collective_id=0, has_side_effects=True, vmem_limit_bytes=VMEM_LIMIT
        ),
        cost_estimate=pl.CostEstimate(
            flops=2 * layers * rows * depth * width * nch,
            bytes_accessed=2 * weights.size + 4 * boards.size,
            transcendentals=0,
        ),
    )(boards, weights.reshape(layers, depth, width), gains, shifts)


def solution(mesh):
    placed = (
        P("dp", None, None, "chan"),
        P(None, None, None, "chan"),
        P(None, "chan"),
        P(None, "chan"),
    )
    return jax.shard_map(
        functools.partial(on_device, mesh.shape["dp"], mesh.shape["chan"]),
        mesh=mesh,
        in_specs=placed,
        out_specs=P("dp", None, None, "chan"),
        check_vma=False,
    )
```

```python
import functools

import jax
import jax.numpy as jnp
from jax import lax
from jax.experimental import pallas as pl
from jax.experimental.pallas import tpu as pltpu
from jax.sharding import PartitionSpec as P

EPSILON = 1e-05
MESH = pl.DeviceIdType.MESH
LANES = 128
VMEM_LIMIT = 52 * 1024 * 1024


def round_up(value, step):
    return -(-value // step) * step


def stack_kernel(
    ndp, nch, side, mine, layers, rows, base,
    boards, weights, affine, out,
    board_own, board_other, wbuf, aff, xf, skip, mask, lhs, zbuf, stats, stage,
    own_sem, a_local, x_send, x_recv, w_local, w_send, w_recv, s_send, s_recv, o_send, o_recv,
):
    dp = lax.axis_index("dp")
    me = lax.axis_index("chan")
    other = 1 - me
    partner = (dp, other)
    total = ndp * nch
    flat_me = dp * nch + me
    stride = side + 1
    points = mine * side * side

    def flip(index, step):
        bit = 1
        while bit <= step:
            if step & bit:
                index = index + bit - 2 * bit * lax.rem(lax.div(index, bit), 2)
            bit *= 2
        return index

    def every_peer(body):
        if total <= 64 and total & (total - 1) == 0:
            for step in range(total - 1, 0, -1):
                flat = flip(flat_me, step)
                body((lax.div(flat, nch), lax.rem(flat, nch)))
        else:
            def one(step, carry):
                flat = lax.rem(flat_me + step, total)
                body((lax.div(flat, nch), lax.rem(flat, nch)))
                return carry
            lax.fori_loop(1, total, one, 0)

    barrier = pltpu.get_barrier_semaphore()
    every_peer(lambda peer: pl.semaphore_signal(barrier, inc=1, device_id=peer, device_id_type=MESH))

    own = pltpu.make_async_copy(boards.at[pl.ds(me * mine, mine)], board_own, own_sem)
    own.start()
    affine_own = pltpu.make_async_copy(affine, aff.at[me], a_local)
    affine_own.start()

    def weight_local(layer):
        return pltpu.make_async_copy(weights.at[layer], wbuf.at[me, layer], w_local.at[layer])

    def weight_remote(layer, half):
        return pltpu.make_async_remote_copy(
            src_ref=weights.at[layer], dst_ref=wbuf.at[half, layer],
            send_sem=w_send.at[layer], recv_sem=w_recv.at[layer],
            device_id=partner, device_id_type=MESH,
        )

    def swap(index, src, dst):
        return pltpu.make_async_remote_copy(
            src_ref=src, dst_ref=dst, send_sem=x_send.at[index], recv_sem=x_recv.at[index],
            device_id=partner, device_id_type=MESH,
        )

    for layer in range(layers):
        weight_local(layer).start()
    xf[...] = jnp.zeros_like(xf)
    mask[...] = jnp.zeros_like(mask)
    for n in range(mine):
        for i in range(side):
            mask[pl.ds((n * stride + i) * stride, side), :] = jnp.ones((side, LANES), jnp.float32)

    pl.semaphore_wait(barrier, total - 1)
    swaps = [
        swap(0, boards.at[pl.ds(other * mine, mine)], board_other),
        swap(1, affine, aff.at[me]),
    ]
    swaps[0].start()
    weight_remote(0, me).start()
    swaps[1].start()

    def place(half, source):
        for n in range(mine):
            for i in range(side):
                at = base + (n * stride + i) * stride
                xf[half, pl.ds(at, side), :] = source[n, i].astype(jnp.float32)

    own.wait()
    place(me, board_own)
    swaps[0].wait_recv()
    place(other, board_other)
    swaps[1].wait_recv()
    affine_own.wait()

    def layer_step(layer, carry):
        odd = lax.rem(layer, 2)

        @pl.when(layer + 1 < layers)
        def _():
            weight_remote(layer + 1, me).start()

        for tap in range(9):
            a, b = divmod(tap, 3)
            at = base + (a - 1) * stride + (b - 1)
            for half in range(nch):
                column = (tap * nch + half) * LANES
                lhs[:, pl.ds(column, LANES)] = xf[half, pl.ds(at, rows), :].astype(jnp.bfloat16)
        weight_local(layer).wait()
        weight_remote(layer, other).wait_recv()
        kernel = jnp.concatenate([wbuf[half, layer] for half in range(nch)], axis=1)
        zbuf[...] = jnp.dot(lhs[...], kernel, preferred_element_type=jnp.float32)

        centre = (side // 2) * stride + side // 2
        for half in range(nch):
            lanes = pl.ds(half * LANES, LANES)
            middle = zbuf[pl.ds(centre, 1), lanes]
            away = (zbuf[:, lanes] - middle) * mask[...]
            first = jnp.sum(away, axis=0, keepdims=True)
            second = jnp.sum(away * away, axis=0, keepdims=True)
            stats[layer, flat_me, pl.ds(half, 1), :] = middle + first * (1.0 / points)
            stats[layer, flat_me, pl.ds(nch + half, 1), :] = second - first * first * (1.0 / points)

        def send(peer):
            pltpu.make_async_remote_copy(
                src_ref=stats.at[layer, flat_me], dst_ref=stats.at[layer, flat_me],
                send_sem=s_send.at[layer], recv_sem=s_recv.at[layer],
                device_id=peer, device_id_type=MESH,
            ).start()

        every_peer(send)

        @pl.when(odd == 0)
        def _():
            for half in range(nch):
                skip[half] = xf[half, pl.ds(base, rows), :]

        arrived = stats.at[layer, pl.ds(0, total - 1)]
        pltpu.make_async_copy(arrived, arrived, s_recv.at[layer]).wait()

        seen = stats[layer]
        mean = jnp.sum(seen, axis=0)[:nch] * (1.0 / total)
        drift = seen[:, :nch] - mean[None]
        var = (jnp.sum(seen[:, nch:], axis=0) + points * jnp.sum(drift * drift, axis=0)) * (1.0 / (points * total))
        inverse = lax.rsqrt(var + EPSILON)
        keep = odd.astype(jnp.float32)
        for half in range(nch):
            gain = aff[half, 0, pl.ds(layer, 1), :] * inverse[half : half + 1]
            shift = aff[half, 1, pl.ds(layer, 1), :]
            normed = (zbuf[:, pl.ds(half * LANES, LANES)] - mean[half : half + 1]) * gain + shift
            normed = normed + skip[half] * keep
            fresh = jnp.maximum(normed, 0.0) * mask[...]
            xf[half, pl.ds(base, rows), :] = fresh.astype(jnp.bfloat16).astype(jnp.float32)
        return carry

    lax.fori_loop(0, layers, layer_step, 0)

    def collect(half, target, first):
        for n in range(mine):
            for i in range(side):
                at = base + (n * stride + i) * stride
                target[first + n, i] = xf[half, pl.ds(at, side), :].astype(jnp.bfloat16)

    collect(other, stage, 0)
    final = pltpu.make_async_remote_copy(
        src_ref=stage, dst_ref=out.at[pl.ds(me * mine, mine)],
        send_sem=o_send, recv_sem=o_recv, device_id=partner, device_id_type=MESH,
    )
    final.start()
    collect(me, out, me * mine)

    for one in swaps:
        one.wait_send()

    def drain(layer, carry):
        weight_remote(layer, me).wait_send()
        sent = stats.at[layer, pl.ds(0, total - 1)]
        pltpu.make_async_copy(sent, sent, s_send.at[layer]).wait()
        return carry

    lax.fori_loop(0, layers, drain, 0)
    final.wait()


def on_device(ndp, nch, boards, weights, gains, shifts):
    held, side, _, width = boards.shape
    layers = weights.shape[0]
    mine = held // nch
    stride = side + 1
    rows = round_up((mine - 1) * stride * stride + side * stride, 16)
    base = round_up(stride + 1, 8)
    span = round_up(base + rows + stride + 1, 8)
    total = ndp * nch
    depth = 9 * width * nch
    dma = pltpu.SemaphoreType.DMA
    in_hbm = pl.BlockSpec(memory_space=pltpu.HBM)
    vmem = pl.BlockSpec(memory_space=pltpu.VMEM)
    return pl.pallas_call(
        functools.partial(stack_kernel, ndp, nch, side, mine, layers, rows, base),
        out_shape=jax.ShapeDtypeStruct(boards.shape, jnp.bfloat16),
        in_specs=[in_hbm] * 3,
        out_specs=vmem,
        scratch_shapes=[
            pltpu.VMEM((mine, side, side, width), jnp.bfloat16),
            pltpu.VMEM((mine, side, side, width), jnp.bfloat16),
            pltpu.VMEM((nch, layers, depth, width), jnp.bfloat16),
            pltpu.VMEM((nch, 2, layers, width), jnp.float32),
            pltpu.VMEM((nch, span, width), jnp.float32),
            pltpu.VMEM((nch, rows, width), jnp.float32),
            pltpu.VMEM((rows, width), jnp.float32),
            pltpu.VMEM((rows, depth), jnp.bfloat16),
            pltpu.VMEM((rows, width * nch), jnp.float32),
            pltpu.VMEM((layers, total, 2 * nch, width), jnp.float32),
            pltpu.VMEM((mine, side, side, width), jnp.bfloat16),
            dma, dma, dma((2,)), dma((2,)),
            dma((layers,)), dma((layers,)), dma((layers,)),
            dma((layers,)), dma((layers,)), dma, dma,
        ],
        compiler_params=pltpu.CompilerParams(
            collective_id=0, has_side_effects=True, vmem_limit_bytes=VMEM_LIMIT
        ),
        cost_estimate=pl.CostEstimate(
            flops=2 * layers * rows * depth * width * nch,
            bytes_accessed=2 * weights.size + 4 * boards.size,
            transcendentals=0,
        ),
    )(boards, weights.reshape(layers, depth, width), jnp.stack([gains, shifts]))


def solution(mesh):
    placed = (
        P("dp", None, None, "chan"),
        P(None, None, None, "chan"),
        P(None, "chan"),
        P(None, "chan"),
    )
    return jax.shard_map(
        functools.partial(on_device, mesh.shape["dp"], mesh.shape["chan"]),
        mesh=mesh,
        in_specs=placed,
        out_specs=P("dp", None, None, "chan"),
        check_vma=False,
    )
```

```python
import functools

import jax
import jax.numpy as jnp
from jax import lax
from jax.experimental import pallas as pl
from jax.experimental.pallas import tpu as pltpu
from jax.sharding import PartitionSpec as P

EPSILON = 1e-05
MESH = pl.DeviceIdType.MESH
LANES = 128
VMEM_LIMIT = 52 * 1024 * 1024


def round_up(value, step):
    return -(-value // step) * step


def stack_kernel(
    ndp, nch, side, mine, layers, rows, base, reach,
    boards, weights, affine, out,
    board_own, board_other, wbuf, aff, xf, skip, mask, shifted, zbuf, stats, stage,
    own_sem, a_local, x_send, x_recv, w_local, w_send, w_recv, s_send, s_recv, o_send, o_recv,
):
    dp = lax.axis_index("dp")
    me = lax.axis_index("chan")
    other = 1 - me
    partner = (dp, other)
    total = ndp * nch
    flat_me = dp * nch + me
    stride = side + 1
    points = mine * side * side

    def flip(index, step):
        bit = 1
        while bit <= step:
            if step & bit:
                index = index + bit - 2 * bit * lax.rem(lax.div(index, bit), 2)
            bit *= 2
        return index

    def every_peer(body):
        if total <= 64 and total & (total - 1) == 0:
            for step in range(total - 1, 0, -1):
                flat = flip(flat_me, step)
                body((lax.div(flat, nch), lax.rem(flat, nch)))
        else:
            def one(step, carry):
                flat = lax.rem(flat_me + step, total)
                body((lax.div(flat, nch), lax.rem(flat, nch)))
                return carry
            lax.fori_loop(1, total, one, 0)

    barrier = pltpu.get_barrier_semaphore()
    every_peer(lambda peer: pl.semaphore_signal(barrier, inc=1, device_id=peer, device_id_type=MESH))

    own = pltpu.make_async_copy(boards.at[pl.ds(me * mine, mine)], board_own, own_sem)
    own.start()
    affine_own = pltpu.make_async_copy(affine, aff.at[me], a_local)
    affine_own.start()

    def weight_local(layer):
        return pltpu.make_async_copy(weights.at[layer], wbuf.at[me, layer], w_local.at[layer])

    def weight_remote(layer, half):
        return pltpu.make_async_remote_copy(
            src_ref=weights.at[layer], dst_ref=wbuf.at[half, layer],
            send_sem=w_send.at[layer], recv_sem=w_recv.at[layer],
            device_id=partner, device_id_type=MESH,
        )

    def swap(index, src, dst):
        return pltpu.make_async_remote_copy(
            src_ref=src, dst_ref=dst, send_sem=x_send.at[index], recv_sem=x_recv.at[index],
            device_id=partner, device_id_type=MESH,
        )

    for layer in range(layers):
        weight_local(layer).start()
    xf[...] = jnp.zeros_like(xf)
    mask[...] = jnp.zeros_like(mask)
    for n in range(mine):
        for i in range(side):
            mask[pl.ds((n * stride + i) * stride, side), :] = jnp.ones((side, LANES), jnp.float32)

    pl.semaphore_wait(barrier, total - 1)
    swaps = [
        swap(0, boards.at[pl.ds(other * mine, mine)], board_other),
        swap(1, affine, aff.at[me]),
    ]
    swaps[0].start()
    weight_remote(0, me).start()
    swaps[1].start()

    def place(half, source):
        for n in range(mine):
            for i in range(side):
                at = base + (n * stride + i) * stride
                xf[half, pl.ds(at, side), :] = source[n, i].astype(jnp.float32)

    own.wait()
    place(me, board_own)
    swaps[0].wait_recv()
    place(other, board_other)
    swaps[1].wait_recv()
    affine_own.wait()

    def layer_step(layer, carry):
        odd = lax.rem(layer, 2)

        @pl.when(layer + 1 < layers)
        def _():
            weight_remote(layer + 1, me).start()

        for b in range(3):
            for half in range(nch):
                shifted[b, half] = xf[half, pl.ds(base - stride + b - 1, reach), :].astype(jnp.bfloat16)
        taps = [
            shifted[tap % 3, half, pl.ds((tap // 3) * stride, rows), :]
            for tap in range(9) for half in range(nch)
        ]
        sample = jnp.concatenate(taps, axis=1)
        weight_local(layer).wait()
        weight_remote(layer, other).wait_recv()
        kernel = jnp.concatenate([wbuf[half, layer] for half in range(nch)], axis=1)
        zbuf[...] = jnp.dot(sample, kernel, preferred_element_type=jnp.float32)

        centre = (side // 2) * stride + side // 2
        for half in range(nch):
            lanes = pl.ds(half * LANES, LANES)
            middle = zbuf[pl.ds(centre, 1), lanes]
            away = (zbuf[:, lanes] - middle) * mask[...]
            first = jnp.sum(away, axis=0, keepdims=True)
            second = jnp.sum(away * away, axis=0, keepdims=True)
            stats[layer, flat_me, pl.ds(half, 1), :] = middle + first * (1.0 / points)
            stats[layer, flat_me, pl.ds(nch + half, 1), :] = second - first * first * (1.0 / points)

        def send(peer):
            pltpu.make_async_remote_copy(
                src_ref=stats.at[layer, flat_me], dst_ref=stats.at[layer, flat_me],
                send_sem=s_send.at[layer], recv_sem=s_recv.at[layer],
                device_id=peer, device_id_type=MESH,
            ).start()

        every_peer(send)

        @pl.when(odd == 0)
        def _():
            for half in range(nch):
                skip[half] = xf[half, pl.ds(base, rows), :]

        arrived = stats.at[layer, pl.ds(0, total - 1)]
        pltpu.make_async_copy(arrived, arrived, s_recv.at[layer]).wait()

        seen = stats[layer]
        mean = jnp.sum(seen, axis=0)[:nch] * (1.0 / total)
        drift = seen[:, :nch] - mean[None]
        var = (jnp.sum(seen[:, nch:], axis=0) + points * jnp.sum(drift * drift, axis=0)) * (1.0 / (points * total))
        inverse = lax.rsqrt(var + EPSILON)
        keep = odd.astype(jnp.float32)
        for half in range(nch):
            gain = aff[half, 0, pl.ds(layer, 1), :] * inverse[half : half + 1]
            shift = aff[half, 1, pl.ds(layer, 1), :]
            normed = (zbuf[:, pl.ds(half * LANES, LANES)] - mean[half : half + 1]) * gain + shift
            normed = normed + skip[half] * keep
            fresh = jnp.maximum(normed, 0.0) * mask[...]
            xf[half, pl.ds(base, rows), :] = fresh.astype(jnp.bfloat16).astype(jnp.float32)
        return carry

    lax.fori_loop(0, layers, layer_step, 0)

    def collect(half, target, first):
        for n in range(mine):
            for i in range(side):
                at = base + (n * stride + i) * stride
                target[first + n, i] = xf[half, pl.ds(at, side), :].astype(jnp.bfloat16)

    collect(other, stage, 0)
    final = pltpu.make_async_remote_copy(
        src_ref=stage, dst_ref=out.at[pl.ds(me * mine, mine)],
        send_sem=o_send, recv_sem=o_recv, device_id=partner, device_id_type=MESH,
    )
    final.start()
    collect(me, out, me * mine)

    for one in swaps:
        one.wait_send()

    def drain(layer, carry):
        weight_remote(layer, me).wait_send()
        sent = stats.at[layer, pl.ds(0, total - 1)]
        pltpu.make_async_copy(sent, sent, s_send.at[layer]).wait()
        return carry

    lax.fori_loop(0, layers, drain, 0)
    final.wait()


def on_device(ndp, nch, boards, weights, gains, shifts):
    held, side, _, width = boards.shape
    layers = weights.shape[0]
    mine = held // nch
    stride = side + 1
    rows = round_up((mine - 1) * stride * stride + side * stride, 16)
    base = round_up(stride + 1, 8)
    reach = round_up(rows + 2 * stride, 16)
    span = round_up(base - stride + 1 + reach, 8)
    total = ndp * nch
    depth = 9 * width * nch
    dma = pltpu.SemaphoreType.DMA
    in_hbm = pl.BlockSpec(memory_space=pltpu.HBM)
    vmem = pl.BlockSpec(memory_space=pltpu.VMEM)
    return pl.pallas_call(
        functools.partial(stack_kernel, ndp, nch, side, mine, layers, rows, base, reach),
        out_shape=jax.ShapeDtypeStruct(boards.shape, jnp.bfloat16),
        in_specs=[in_hbm] * 3,
        out_specs=vmem,
        scratch_shapes=[
            pltpu.VMEM((mine, side, side, width), jnp.bfloat16),
            pltpu.VMEM((mine, side, side, width), jnp.bfloat16),
            pltpu.VMEM((nch, layers, depth, width), jnp.bfloat16),
            pltpu.VMEM((nch, 2, layers, width), jnp.float32),
            pltpu.VMEM((nch, span, width), jnp.float32),
            pltpu.VMEM((nch, rows, width), jnp.float32),
            pltpu.VMEM((rows, width), jnp.float32),
            pltpu.VMEM((3, nch, reach, width), jnp.bfloat16),
            pltpu.VMEM((rows, width * nch), jnp.float32),
            pltpu.VMEM((layers, total, 2 * nch, width), jnp.float32),
            pltpu.VMEM((mine, side, side, width), jnp.bfloat16),
            dma, dma, dma((2,)), dma((2,)),
            dma((layers,)), dma((layers,)), dma((layers,)),
            dma((layers,)), dma((layers,)), dma, dma,
        ],
        compiler_params=pltpu.CompilerParams(
            collective_id=0, has_side_effects=True, vmem_limit_bytes=VMEM_LIMIT
        ),
        cost_estimate=pl.CostEstimate(
            flops=2 * layers * rows * depth * width * nch,
            bytes_accessed=2 * weights.size + 4 * boards.size,
            transcendentals=0,
        ),
    )(boards, weights.reshape(layers, depth, width), jnp.stack([gains, shifts]))


def solution(mesh):
    placed = (
        P("dp", None, None, "chan"),
        P(None, None, None, "chan"),
        P(None, "chan"),
        P(None, "chan"),
    )
    return jax.shard_map(
        functools.partial(on_device, mesh.shape["dp"], mesh.shape["chan"]),
        mesh=mesh,
        in_specs=placed,
        out_specs=P("dp", None, None, "chan"),
        check_vma=False,
    )
```

```python
import functools

import jax
import jax.numpy as jnp
from jax import lax
from jax.experimental import pallas as pl
from jax.experimental.pallas import tpu as pltpu
from jax.sharding import PartitionSpec as P

EPSILON = 1e-05
MESH = pl.DeviceIdType.MESH
LANES = 128
VMEM_LIMIT = 52 * 1024 * 1024


def round_up(value, step):
    return -(-value // step) * step


def stack_kernel(
    ndp, nch, side, mine, layers, rows, base,
    boards, weights, affine, out,
    raw, board_send, board_other, wbuf, aff, xf, skip, mask, lhs, zbuf, stats, stage,
    own_sem, a_local, x_send, x_recv, w_local, w_send, w_recv, s_send, s_recv, o_send, o_recv,
):
    dp = lax.axis_index("dp")
    me = lax.axis_index("chan")
    other = 1 - me
    partner = (dp, other)
    total = ndp * nch
    flat_me = dp * nch + me
    stride = side + 1
    points = mine * side * side

    def flip(index, step):
        bit = 1
        while bit <= step:
            if step & bit:
                index = index + bit - 2 * bit * lax.rem(lax.div(index, bit), 2)
            bit *= 2
        return index

    def every_peer(body):
        if total <= 64 and total & (total - 1) == 0:
            for step in range(total - 1, 0, -1):
                flat = flip(flat_me, step)
                body((lax.div(flat, nch), lax.rem(flat, nch)))
        else:
            def one(step, carry):
                flat = lax.rem(flat_me + step, total)
                body((lax.div(flat, nch), lax.rem(flat, nch)))
                return carry
            lax.fori_loop(1, total, one, 0)

    barrier = pltpu.get_barrier_semaphore()
    every_peer(lambda peer: pl.semaphore_signal(barrier, inc=1, device_id=peer, device_id_type=MESH))

    own = pltpu.make_async_copy(boards, raw, own_sem)
    own.start()
    affine_own = pltpu.make_async_copy(affine, aff.at[me], a_local)
    affine_own.start()

    def weight_local(layer):
        return pltpu.make_async_copy(weights.at[layer], wbuf.at[me, layer], w_local.at[layer])

    def weight_remote(layer, half):
        return pltpu.make_async_remote_copy(
            src_ref=weights.at[layer], dst_ref=wbuf.at[half, layer],
            send_sem=w_send.at[layer], recv_sem=w_recv.at[layer],
            device_id=partner, device_id_type=MESH,
        )

    def swap(index, src, dst):
        return pltpu.make_async_remote_copy(
            src_ref=src, dst_ref=dst, send_sem=x_send.at[index], recv_sem=x_recv.at[index],
            device_id=partner, device_id_type=MESH,
        )

    for layer in range(layers):
        weight_local(layer).start()
    xf[...] = jnp.zeros_like(xf)
    mask[...] = jnp.zeros_like(mask)
    for n in range(mine):
        for i in range(side):
            mask[pl.ds((n * stride + i) * stride, side), :] = jnp.ones((side, LANES), jnp.float32)

    own.wait()
    for i in range(side):
        line = raw[i].astype(jnp.float32)
        for n in range(mine):
            at = base + (n * stride + i) * stride
            planes = [line[:, half * mine + n, :] for half in range(nch)]
            kept = jnp.where(me == 0, planes[0], planes[1])
            given = jnp.where(me == 0, planes[1], planes[0])
            xf[me, pl.ds(at, side), :] = kept
            board_send[n, i] = given.astype(jnp.bfloat16)

    pl.semaphore_wait(barrier, total - 1)
    swaps = [
        swap(0, board_send, board_other),
        swap(1, affine, aff.at[me]),
    ]
    swaps[0].start()
    weight_remote(0, me).start()
    swaps[1].start()

    def place(half, source):
        for n in range(mine):
            for i in range(side):
                at = base + (n * stride + i) * stride
                xf[half, pl.ds(at, side), :] = source[n, i].astype(jnp.float32)

    swaps[0].wait_recv()
    place(other, board_other)
    swaps[1].wait_recv()
    affine_own.wait()

    def layer_step(layer, carry):
        odd = lax.rem(layer, 2)

        @pl.when(layer + 1 < layers)
        def _():
            weight_remote(layer + 1, me).start()

        for tap in range(9):
            a, b = divmod(tap, 3)
            at = base + (a - 1) * stride + (b - 1)
            for half in range(nch):
                column = (tap * nch + half) * LANES
                lhs[:, pl.ds(column, LANES)] = xf[half, pl.ds(at, rows), :].astype(jnp.bfloat16)
        weight_local(layer).wait()
        weight_remote(layer, other).wait_recv()
        kernel = jnp.concatenate([wbuf[half, layer] for half in range(nch)], axis=1)
        zbuf[...] = jnp.dot(lhs[...], kernel, preferred_element_type=jnp.float32)

        centre = (side // 2) * stride + side // 2
        for half in range(nch):
            lanes = pl.ds(half * LANES, LANES)
            middle = zbuf[pl.ds(centre, 1), lanes]
            away = (zbuf[:, lanes] - middle) * mask[...]
            first = jnp.sum(away, axis=0, keepdims=True)
            second = jnp.sum(away * away, axis=0, keepdims=True)
            stats[layer, flat_me, pl.ds(half, 1), :] = middle + first * (1.0 / points)
            stats[layer, flat_me, pl.ds(nch + half, 1), :] = second - first * first * (1.0 / points)

        def send(peer):
            pltpu.make_async_remote_copy(
                src_ref=stats.at[layer, flat_me], dst_ref=stats.at[layer, flat_me],
                send_sem=s_send.at[layer], recv_sem=s_recv.at[layer],
                device_id=peer, device_id_type=MESH,
            ).start()

        every_peer(send)

        @pl.when(odd == 0)
        def _():
            for half in range(nch):
                skip[half] = xf[half, pl.ds(base, rows), :]

        arrived = stats.at[layer, pl.ds(0, total - 1)]
        pltpu.make_async_copy(arrived, arrived, s_recv.at[layer]).wait()

        seen = stats[layer]
        mine_mean = stats[layer, flat_me, pl.ds(0, nch), :]
        drift = seen[:, :nch] - mine_mean[None]
        shifted = jnp.sum(drift, axis=0)
        spread = jnp.sum(points * drift * drift + seen[:, nch:], axis=0)
        mean = mine_mean + shifted * (1.0 / total)
        var = (spread - shifted * shifted * (points / total)) * (1.0 / (points * total))
        inverse = lax.rsqrt(var + EPSILON)
        keep = odd.astype(jnp.float32)
        for half in range(nch):
            gain = aff[half, 0, pl.ds(layer, 1), :] * inverse[half : half + 1]
            shift = aff[half, 1, pl.ds(layer, 1), :]
            normed = (zbuf[:, pl.ds(half * LANES, LANES)] - mean[half : half + 1]) * gain + shift
            normed = normed + skip[half] * keep
            fresh = jnp.maximum(normed, 0.0) * mask[...]
            xf[half, pl.ds(base, rows), :] = fresh.astype(jnp.bfloat16).astype(jnp.float32)
        return carry

    lax.fori_loop(0, layers, layer_step, 0)

    def collect(half, target, first):
        for n in range(mine):
            for i in range(side):
                at = base + (n * stride + i) * stride
                target[first + n, i] = xf[half, pl.ds(at, side), :].astype(jnp.bfloat16)

    collect(other, stage, 0)
    final = pltpu.make_async_remote_copy(
        src_ref=stage, dst_ref=out.at[pl.ds(me * mine, mine)],
        send_sem=o_send, recv_sem=o_recv, device_id=partner, device_id_type=MESH,
    )
    final.start()
    collect(me, out, me * mine)

    for one in swaps:
        one.wait_send()

    def drain(layer, carry):
        weight_remote(layer, me).wait_send()
        sent = stats.at[layer, pl.ds(0, total - 1)]
        pltpu.make_async_copy(sent, sent, s_send.at[layer]).wait()
        return carry

    lax.fori_loop(0, layers, drain, 0)
    final.wait()


def on_device(ndp, nch, boards, weights, gains, shifts):
    held, side, _, width = boards.shape
    layers = weights.shape[0]
    mine = held // nch
    stride = side + 1
    rows = round_up((mine - 1) * stride * stride + side * stride, 16)
    base = round_up(stride + 1, 8)
    span = round_up(base + rows + stride + 1, 8)
    total = ndp * nch
    depth = 9 * width * nch
    dma = pltpu.SemaphoreType.DMA
    in_hbm = pl.BlockSpec(memory_space=pltpu.HBM)
    vmem = pl.BlockSpec(memory_space=pltpu.VMEM)
    return pl.pallas_call(
        functools.partial(stack_kernel, ndp, nch, side, mine, layers, rows, base),
        out_shape=jax.ShapeDtypeStruct(boards.shape, jnp.bfloat16),
        in_specs=[in_hbm] * 3,
        out_specs=vmem,
        scratch_shapes=[
            pltpu.VMEM((side, side, held, width), jnp.bfloat16),
            pltpu.VMEM((mine, side, side, width), jnp.bfloat16),
            pltpu.VMEM((mine, side, side, width), jnp.bfloat16),
            pltpu.VMEM((nch, layers, depth, width), jnp.bfloat16),
            pltpu.VMEM((nch, 2, layers, width), jnp.float32),
            pltpu.VMEM((nch, span, width), jnp.float32),
            pltpu.VMEM((nch, rows, width), jnp.float32),
            pltpu.VMEM((rows, width), jnp.float32),
            pltpu.VMEM((rows, depth), jnp.bfloat16),
            pltpu.VMEM((rows, width * nch), jnp.float32),
            pltpu.VMEM((layers, total, 2 * nch, width), jnp.float32),
            pltpu.VMEM((mine, side, side, width), jnp.bfloat16),
            dma, dma, dma((2,)), dma((2,)),
            dma((layers,)), dma((layers,)), dma((layers,)),
            dma((layers,)), dma((layers,)), dma, dma,
        ],
        compiler_params=pltpu.CompilerParams(
            collective_id=0, has_side_effects=True, vmem_limit_bytes=VMEM_LIMIT
        ),
        cost_estimate=pl.CostEstimate(
            flops=2 * layers * rows * depth * width * nch,
            bytes_accessed=2 * weights.size + 4 * boards.size,
            transcendentals=0,
        ),
    )(boards.transpose(1, 2, 0, 3), weights.reshape(layers, depth, width), jnp.stack([gains, shifts]))


def solution(mesh):
    placed = (
        P("dp", None, None, "chan"),
        P(None, None, None, "chan"),
        P(None, "chan"),
        P(None, "chan"),
    )
    return jax.shard_map(
        functools.partial(on_device, mesh.shape["dp"], mesh.shape["chan"]),
        mesh=mesh,
        in_specs=placed,
        out_specs=P("dp", None, None, "chan"),
        check_vma=False,
    )
```

```python
import functools

import jax
import jax.numpy as jnp
from jax import lax
from jax.experimental import pallas as pl
from jax.experimental.pallas import tpu as pltpu
from jax.sharding import PartitionSpec as P

EPSILON = 1e-05
MESH = pl.DeviceIdType.MESH
LANES = 128
VMEM_LIMIT = 57 * 1024 * 1024


def round_up(value, step):
    return -(-value // step) * step


def stack_kernel(
    ndp, nch, side, mine, layers, rows, base,
    boards, weights, gains, shifts, out,
    raw, board_send, board_other, wbuf, aff, xf, skip, mask, lhs, zbuf, stats, stage, stage_own,
    own_sem, a_local, x_send, x_recv, w_local, w_send, w_recv, s_send, s_recv, o_send, o_recv,
):
    dp = lax.axis_index("dp")
    me = lax.axis_index("chan")
    other = 1 - me
    partner = (dp, other)
    total = ndp * nch
    flat_me = dp * nch + me
    stride = side + 1
    points = mine * side * side

    def flip(index, step):
        bit = 1
        while bit <= step:
            if step & bit:
                index = index + bit - 2 * bit * lax.rem(lax.div(index, bit), 2)
            bit *= 2
        return index

    def every_peer(body):
        if total <= 64 and total & (total - 1) == 0:
            for step in range(total - 1, 0, -1):
                flat = flip(flat_me, step)
                body((lax.div(flat, nch), lax.rem(flat, nch)))
        else:
            def one(step, carry):
                flat = lax.rem(flat_me + step, total)
                body((lax.div(flat, nch), lax.rem(flat, nch)))
                return carry
            lax.fori_loop(1, total, one, 0)

    barrier = pltpu.get_barrier_semaphore()
    every_peer(lambda peer: pl.semaphore_signal(barrier, inc=1, device_id=peer, device_id_type=MESH))

    own = pltpu.make_async_copy(boards, raw, own_sem)
    own.start()
    affine_own = [
        pltpu.make_async_copy(gains, aff.at[me, 0], a_local.at[0]),
        pltpu.make_async_copy(shifts, aff.at[me, 1], a_local.at[1]),
    ]
    for one in affine_own:
        one.start()

    def weight_local(layer):
        return pltpu.make_async_copy(weights.at[layer], wbuf.at[me, layer], w_local.at[layer])

    def weight_remote(layer, half):
        return pltpu.make_async_remote_copy(
            src_ref=weights.at[layer], dst_ref=wbuf.at[half, layer],
            send_sem=w_send.at[layer], recv_sem=w_recv.at[layer],
            device_id=partner, device_id_type=MESH,
        )

    def swap(index, src, dst):
        return pltpu.make_async_remote_copy(
            src_ref=src, dst_ref=dst, send_sem=x_send.at[index], recv_sem=x_recv.at[index],
            device_id=partner, device_id_type=MESH,
        )

    for layer in range(layers):
        weight_local(layer).start()
    xf[...] = jnp.zeros_like(xf)
    mask[...] = jnp.zeros_like(mask)
    for n in range(mine):
        for i in range(side):
            mask[pl.ds((n * stride + i) * stride, side), :] = jnp.ones((side, LANES), jnp.float32)

    own.wait()
    for i in range(side):
        line = raw[i].astype(jnp.float32)
        for n in range(mine):
            at = base + (n * stride + i) * stride
            planes = [line[:, half * mine + n, :] for half in range(nch)]
            kept = jnp.where(me == 0, planes[0], planes[1])
            given = jnp.where(me == 0, planes[1], planes[0])
            xf[me, pl.ds(at, side), :] = kept
            board_send[n, i] = given.astype(jnp.bfloat16)

    pl.semaphore_wait(barrier, total - 1)
    swaps = [
        swap(0, board_send, board_other),
        swap(1, gains, aff.at[me, 0]),
        swap(2, shifts, aff.at[me, 1]),
    ]
    swaps[0].start()
    weight_remote(0, me).start()
    swaps[1].start()
    swaps[2].start()

    def place(half, source):
        for n in range(mine):
            for i in range(side):
                at = base + (n * stride + i) * stride
                xf[half, pl.ds(at, side), :] = source[n, i].astype(jnp.float32)

    swaps[0].wait_recv()
    place(other, board_other)
    swaps[1].wait_recv()
    swaps[2].wait_recv()
    for one in affine_own:
        one.wait()

    def parity(layer):
        return layer % 2 if isinstance(layer, int) else lax.rem(layer, 2)

    def send_stats(layer):
        centre = (side // 2) * stride + side // 2
        for half in range(nch):
            lanes = pl.ds(half * LANES, LANES)
            middle = zbuf[pl.ds(centre, 1), lanes]
            away = (zbuf[:, lanes] - middle) * mask[...]
            first = jnp.sum(away, axis=0, keepdims=True)
            second = jnp.sum(away * away, axis=0, keepdims=True)
            stats[layer, flat_me, pl.ds(half, 1), :] = middle + first * (1.0 / points)
            stats[layer, flat_me, pl.ds(nch + half, 1), :] = second - first * first * (1.0 / points)

        def send(peer):
            pltpu.make_async_remote_copy(
                src_ref=stats.at[layer, flat_me], dst_ref=stats.at[layer, flat_me],
                send_sem=s_send.at[layer], recv_sem=s_recv.at[layer],
                device_id=peer, device_id_type=MESH,
            ).start()

        every_peer(send)

        @pl.when(parity(layer) == 0)
        def _():
            for half in range(nch):
                skip[half] = xf[half, pl.ds(base, rows), :]

    def merged(layer):
        arrived = stats.at[layer, pl.ds(0, total - 1)]
        pltpu.make_async_copy(arrived, arrived, s_recv.at[layer]).wait()
        seen = stats[layer]
        mine_mean = stats[layer, flat_me, pl.ds(0, nch), :]
        drift = seen[:, :nch] - mine_mean[None]
        shifted = jnp.sum(drift, axis=0)
        spread = jnp.sum(points * drift * drift + seen[:, nch:], axis=0)
        mean = mine_mean + shifted * (1.0 / total)
        var = (spread - shifted * shifted * (points / total)) * (1.0 / (points * total))
        return mean, lax.rsqrt(var + EPSILON)

    def normalise(layer, half, mean, inverse):
        keep = 1.0 * parity(layer)
        gain = aff[half, 0, pl.ds(layer, 1), :] * inverse[half : half + 1]
        shift = aff[half, 1, pl.ds(layer, 1), :]
        normed = (zbuf[:, pl.ds(half * LANES, LANES)] - mean[half : half + 1]) * gain + shift
        normed = normed + skip[half] * keep
        fresh = jnp.maximum(normed, 0.0) * mask[...]
        xf[half, pl.ds(base, rows), :] = fresh.astype(jnp.bfloat16).astype(jnp.float32)

    def multiply(layer, half):
        for tap in range(9):
            a, b = divmod(tap, 3)
            at = base + (a - 1) * stride + (b - 1)
            lhs[half, :, pl.ds(tap * LANES, LANES)] = xf[half, pl.ds(at, rows), :].astype(jnp.bfloat16)
        kernel = jnp.concatenate([
            jnp.concatenate([
                wbuf[column, layer, pl.ds((tap * nch + half) * LANES, LANES), :] for column in range(nch)
            ], axis=1)
            for tap in range(9)
        ], axis=0)
        return jnp.dot(lhs[half], kernel, preferred_element_type=jnp.float32)

    def weights_ready(layer):
        weight_local(layer).wait()
        weight_remote(layer, other).wait_recv()

    if layers > 1:
        weight_remote(1, me).start()
    weights_ready(0)
    zbuf[...] = sum(multiply(0, half) for half in range(nch))
    send_stats(0)

    def layer_step(layer, carry):
        @pl.when(layer + 1 < layers)
        def _():
            weight_remote(layer + 1, me).start()

        weights_ready(layer)
        mean, inverse = merged(layer - 1)
        parts = []
        for half in range(nch):
            normalise(layer - 1, half, mean, inverse)
            parts.append(multiply(layer, half))
        zbuf[...] = sum(parts)
        send_stats(layer)
        return carry

    lax.fori_loop(1, layers, layer_step, 0)
    mean, inverse = merged(layers - 1)
    for half in range(nch):
        normalise(layers - 1, half, mean, inverse)

    def collect(half, target, first):
        for n in range(mine):
            for i in range(side):
                at = base + (n * stride + i) * stride
                target[first + n, i] = xf[half, pl.ds(at, side), :].astype(jnp.bfloat16)

    collect(other, stage, 0)
    final = pltpu.make_async_remote_copy(
        src_ref=stage, dst_ref=out.at[pl.ds(me * mine, mine)],
        send_sem=o_send, recv_sem=o_recv, device_id=partner, device_id_type=MESH,
    )
    final.start()
    collect(me, stage_own, 0)
    kept = pltpu.make_async_copy(stage_own, out.at[pl.ds(me * mine, mine)], own_sem)
    kept.start()

    for one in swaps:
        one.wait_send()

    def drain(layer, carry):
        weight_remote(layer, me).wait_send()
        sent = stats.at[layer, pl.ds(0, total - 1)]
        pltpu.make_async_copy(sent, sent, s_send.at[layer]).wait()
        return carry

    lax.fori_loop(0, layers, drain, 0)
    kept.wait()
    final.wait()


def on_device(ndp, nch, boards, weights, gains, shifts):
    held, side, _, width = boards.shape
    layers = weights.shape[0]
    mine = held // nch
    stride = side + 1
    rows = round_up((mine - 1) * stride * stride + side * stride, 16)
    base = round_up(stride + 1, 8)
    span = round_up(base + rows + stride + 1, 8)
    total = ndp * nch
    depth = 9 * width * nch
    dma = pltpu.SemaphoreType.DMA
    in_hbm = pl.BlockSpec(memory_space=pltpu.HBM)
    return pl.pallas_call(
        functools.partial(stack_kernel, ndp, nch, side, mine, layers, rows, base),
        out_shape=jax.ShapeDtypeStruct(boards.shape, jnp.bfloat16),
        in_specs=[in_hbm] * 4,
        out_specs=in_hbm,
        scratch_shapes=[
            pltpu.VMEM((side, side, held, width), jnp.bfloat16),
            pltpu.VMEM((mine, side, side, width), jnp.bfloat16),
            pltpu.VMEM((mine, side, side, width), jnp.bfloat16),
            pltpu.VMEM((nch, layers, depth, width), jnp.bfloat16),
            pltpu.VMEM((nch, 2, layers, width), jnp.float32),
            pltpu.VMEM((nch, span, width), jnp.float32),
            pltpu.VMEM((nch, rows, width), jnp.float32),
            pltpu.VMEM((rows, width), jnp.float32),
            pltpu.VMEM((nch, rows, depth // nch), jnp.bfloat16),
            pltpu.VMEM((rows, width * nch), jnp.float32),
            pltpu.VMEM((layers, total, 2 * nch, width), jnp.float32),
            pltpu.VMEM((mine, side, side, width), jnp.bfloat16),
            pltpu.VMEM((mine, side, side, width), jnp.bfloat16),
            dma, dma((2,)), dma((3,)), dma((3,)),
            dma((layers,)), dma((layers,)), dma((layers,)),
            dma((layers,)), dma((layers,)), dma, dma,
        ],
        compiler_params=pltpu.CompilerParams(
            collective_id=0, has_side_effects=True, vmem_limit_bytes=VMEM_LIMIT
        ),
        cost_estimate=pl.CostEstimate(
            flops=2 * layers * rows * depth * width * nch,
            bytes_accessed=2 * weights.size + 4 * boards.size,
            transcendentals=0,
        ),
    )(boards.transpose(1, 2, 0, 3), weights.reshape(layers, depth, width), gains, shifts)


def solution(mesh):
    placed = (
        P("dp", None, None, "chan"),
        P(None, None, None, "chan"),
        P(None, "chan"),
        P(None, "chan"),
    )
    return jax.shard_map(
        functools.partial(on_device, mesh.shape["dp"], mesh.shape["chan"]),
        mesh=mesh,
        in_specs=placed,
        out_specs=P("dp", None, None, "chan"),
        check_vma=False,
    )
```

```python
import functools

import jax
import jax.numpy as jnp
from jax import lax
from jax.experimental import pallas as pl
from jax.experimental.pallas import tpu as pltpu
from jax.sharding import PartitionSpec as P

EPSILON = 1e-05
MESH = pl.DeviceIdType.MESH
LANES = 128
VMEM_LIMIT = 57 * 1024 * 1024


def round_up(value, step):
    return -(-value // step) * step


def stack_kernel(
    ndp, nch, side, mine, layers, rows, base,
    boards, weights, gains, shifts, out,
    raw, board_send, board_other, wbuf, aff, xf, skip, mask, lhs, zbuf, stats, stage, stage_own,
    own_sem, a_local, x_send, x_recv, w_local, w_send, w_recv, s_send, s_recv, o_send, o_recv,
):
    dp = lax.axis_index("dp")
    me = lax.axis_index("chan")
    other = 1 - me
    partner = (dp, other)
    total = ndp * nch
    flat_me = dp * nch + me
    stride = side + 1
    points = mine * side * side

    def flip(index, step):
        bit = 1
        while bit <= step:
            if step & bit:
                index = index + bit - 2 * bit * lax.rem(lax.div(index, bit), 2)
            bit *= 2
        return index

    def every_peer(body):
        if total <= 64 and total & (total - 1) == 0:
            for step in range(total - 1, 0, -1):
                flat = flip(flat_me, step)
                body((lax.div(flat, nch), lax.rem(flat, nch)))
        else:
            def one(step, carry):
                flat = lax.rem(flat_me + step, total)
                body((lax.div(flat, nch), lax.rem(flat, nch)))
                return carry
            lax.fori_loop(1, total, one, 0)

    barrier = pltpu.get_barrier_semaphore()
    every_peer(lambda peer: pl.semaphore_signal(barrier, inc=1, device_id=peer, device_id_type=MESH))

    own = pltpu.make_async_copy(boards, raw, own_sem)
    own.start()
    affine_own = [
        pltpu.make_async_copy(gains, aff.at[me, 0], a_local.at[0]),
        pltpu.make_async_copy(shifts, aff.at[me, 1], a_local.at[1]),
    ]
    for one in affine_own:
        one.start()

    def weight_local(layer):
        return pltpu.make_async_copy(weights.at[layer], wbuf.at[me, layer], w_local.at[layer])

    def weight_remote(layer, half):
        return pltpu.make_async_remote_copy(
            src_ref=weights.at[layer], dst_ref=wbuf.at[half, layer],
            send_sem=w_send.at[layer], recv_sem=w_recv.at[layer],
            device_id=partner, device_id_type=MESH,
        )

    def swap(index, src, dst):
        return pltpu.make_async_remote_copy(
            src_ref=src, dst_ref=dst, send_sem=x_send.at[index], recv_sem=x_recv.at[index],
            device_id=partner, device_id_type=MESH,
        )

    for layer in range(layers):
        weight_local(layer).start()
    xf[...] = jnp.zeros_like(xf)
    mask[...] = jnp.zeros_like(mask)
    for n in range(mine):
        for i in range(side):
            mask[pl.ds((n * stride + i) * stride, side), :] = jnp.ones((side, LANES), jnp.float32)

    own.wait()
    for i in range(side):
        line = raw[i].astype(jnp.float32)
        for n in range(mine):
            at = base + (n * stride + i) * stride
            planes = [line[:, half * mine + n, :] for half in range(nch)]
            kept = jnp.where(me == 0, planes[0], planes[1])
            given = jnp.where(me == 0, planes[1], planes[0])
            xf[me, pl.ds(at, side), :] = kept
            board_send[n, i] = given.astype(jnp.bfloat16)

    pl.semaphore_wait(barrier, total - 1)
    swaps = [
        swap(0, board_send, board_other),
        swap(1, gains, aff.at[me, 0]),
        swap(2, shifts, aff.at[me, 1]),
    ]
    swaps[0].start()
    weight_remote(0, me).start()
    swaps[1].start()
    swaps[2].start()

    def place(half, source):
        for n in range(mine):
            for i in range(side):
                at = base + (n * stride + i) * stride
                xf[half, pl.ds(at, side), :] = source[n, i].astype(jnp.float32)

    swaps[0].wait_recv()
    place(other, board_other)
    swaps[1].wait_recv()
    swaps[2].wait_recv()
    for one in affine_own:
        one.wait()

    def parity(layer):
        return layer % 2 if isinstance(layer, int) else lax.rem(layer, 2)

    def send_stats(layer):
        centre = (side // 2) * stride + side // 2
        for half in range(nch):
            lanes = pl.ds(half * LANES, LANES)
            middle = zbuf[pl.ds(centre, 1), lanes]
            away = (zbuf[:, lanes] - middle) * mask[...]
            first = jnp.sum(away, axis=0, keepdims=True)
            second = jnp.sum(away * away, axis=0, keepdims=True)
            stats[layer, flat_me, pl.ds(half, 1), :] = middle + first * (1.0 / points)
            stats[layer, flat_me, pl.ds(nch + half, 1), :] = second - first * first * (1.0 / points)

        def send(peer):
            pltpu.make_async_remote_copy(
                src_ref=stats.at[layer, flat_me], dst_ref=stats.at[layer, flat_me],
                send_sem=s_send.at[layer], recv_sem=s_recv.at[layer],
                device_id=peer, device_id_type=MESH,
            ).start()

        every_peer(send)

        @pl.when(parity(layer) == 0)
        def _():
            for half in range(nch):
                skip[half] = xf[half, pl.ds(base, rows), :]

    def merged(layer):
        arrived = stats.at[layer, pl.ds(0, total - 1)]
        pltpu.make_async_copy(arrived, arrived, s_recv.at[layer]).wait()
        seen = stats[layer]
        mine_mean = stats[layer, flat_me, pl.ds(0, nch), :]
        drift = seen[:, :nch] - mine_mean[None]
        shifted = jnp.sum(drift, axis=0)
        spread = jnp.sum(points * drift * drift + seen[:, nch:], axis=0)
        mean = mine_mean + shifted * (1.0 / total)
        var = (spread - shifted * shifted * (points / total)) * (1.0 / (points * total))
        return mean, lax.rsqrt(var + EPSILON)

    def normalise(layer, half, mean, inverse):
        keep = 1.0 * parity(layer)
        gain = aff[half, 0, pl.ds(layer, 1), :] * inverse[half : half + 1]
        shift = aff[half, 1, pl.ds(layer, 1), :]
        normed = (zbuf[:, pl.ds(half * LANES, LANES)] - mean[half : half + 1]) * gain + shift
        normed = normed + skip[half] * keep
        fresh = jnp.maximum(normed, 0.0) * mask[...]
        xf[half, pl.ds(base, rows), :] = fresh.astype(jnp.bfloat16).astype(jnp.float32)

    def window(half):
        for tap in range(9):
            a, b = divmod(tap, 3)
            at = base + (a - 1) * stride + (b - 1)
            lhs[half, :, pl.ds(tap * LANES, LANES)] = xf[half, pl.ds(at, rows), :].astype(jnp.bfloat16)

    def product(layer, half, columns):
        kernel = jnp.concatenate([
            jnp.concatenate([
                wbuf[column, layer, pl.ds((tap * nch + half) * LANES, LANES), :] for column in columns
            ], axis=1)
            for tap in range(9)
        ], axis=0)
        return jnp.dot(lhs[half], kernel, preferred_element_type=jnp.float32)

    def weights_ready(layer):
        weight_local(layer).wait()
        weight_remote(layer, other).wait_recv()

    if layers > 1:
        weight_remote(1, me).start()
    for half in range(nch):
        window(half)
    weight_local(0).wait()
    for column in (me, other):
        if column is other:
            weight_remote(0, other).wait_recv()
        lanes = pl.ds(pl.multiple_of(column * LANES, LANES), LANES)
        zbuf[:, lanes] = sum(product(0, half, [column]) for half in range(nch))
    send_stats(0)

    def layer_step(layer, carry):
        @pl.when(layer + 1 < layers)
        def _():
            weight_remote(layer + 1, me).start()

        weights_ready(layer)
        mean, inverse = merged(layer - 1)
        parts = []
        for half in range(nch):
            normalise(layer - 1, half, mean, inverse)
            window(half)
            parts.append(product(layer, half, range(nch)))
        zbuf[...] = sum(parts)
        send_stats(layer)
        return carry

    lax.fori_loop(1, layers, layer_step, 0)
    mean, inverse = merged(layers - 1)
    for half in range(nch):
        normalise(layers - 1, half, mean, inverse)

    def collect(half, target, first):
        for n in range(mine):
            for i in range(side):
                at = base + (n * stride + i) * stride
                target[first + n, i] = xf[half, pl.ds(at, side), :].astype(jnp.bfloat16)

    collect(other, stage, 0)
    final = pltpu.make_async_remote_copy(
        src_ref=stage, dst_ref=out.at[pl.ds(me * mine, mine)],
        send_sem=o_send, recv_sem=o_recv, device_id=partner, device_id_type=MESH,
    )
    final.start()
    collect(me, stage_own, 0)
    kept = pltpu.make_async_copy(stage_own, out.at[pl.ds(me * mine, mine)], own_sem)
    kept.start()

    for one in swaps:
        one.wait_send()

    def drain(layer, carry):
        weight_remote(layer, me).wait_send()
        sent = stats.at[layer, pl.ds(0, total - 1)]
        pltpu.make_async_copy(sent, sent, s_send.at[layer]).wait()
        return carry

    lax.fori_loop(0, layers, drain, 0)
    kept.wait()
    final.wait()


def on_device(ndp, nch, boards, weights, gains, shifts):
    held, side, _, width = boards.shape
    layers = weights.shape[0]
    mine = held // nch
    stride = side + 1
    rows = round_up((mine - 1) * stride * stride + side * stride, 16)
    base = round_up(stride + 1, 8)
    span = round_up(base + rows + stride + 1, 8)
    total = ndp * nch
    depth = 9 * width * nch
    dma = pltpu.SemaphoreType.DMA
    in_hbm = pl.BlockSpec(memory_space=pltpu.HBM)
    return pl.pallas_call(
        functools.partial(stack_kernel, ndp, nch, side, mine, layers, rows, base),
        out_shape=jax.ShapeDtypeStruct(boards.shape, jnp.bfloat16),
        in_specs=[in_hbm] * 4,
        out_specs=in_hbm,
        scratch_shapes=[
            pltpu.VMEM((side, side, held, width), jnp.bfloat16),
            pltpu.VMEM((mine, side, side, width), jnp.bfloat16),
            pltpu.VMEM((mine, side, side, width), jnp.bfloat16),
            pltpu.VMEM((nch, layers, depth, width), jnp.bfloat16),
            pltpu.VMEM((nch, 2, layers, width), jnp.float32),
            pltpu.VMEM((nch, span, width), jnp.float32),
            pltpu.VMEM((nch, rows, width), jnp.float32),
            pltpu.VMEM((rows, width), jnp.float32),
            pltpu.VMEM((nch, rows, depth // nch), jnp.bfloat16),
            pltpu.VMEM((rows, width * nch), jnp.float32),
            pltpu.VMEM((layers, total, 2 * nch, width), jnp.float32),
            pltpu.VMEM((mine, side, side, width), jnp.bfloat16),
            pltpu.VMEM((mine, side, side, width), jnp.bfloat16),
            dma, dma((2,)), dma((3,)), dma((3,)),
            dma((layers,)), dma((layers,)), dma((layers,)),
            dma((layers,)), dma((layers,)), dma, dma,
        ],
        compiler_params=pltpu.CompilerParams(
            collective_id=0, has_side_effects=True, vmem_limit_bytes=VMEM_LIMIT
        ),
        cost_estimate=pl.CostEstimate(
            flops=2 * layers * rows * depth * width * nch,
            bytes_accessed=2 * weights.size + 4 * boards.size,
            transcendentals=0,
        ),
    )(boards.transpose(1, 2, 0, 3), weights.reshape(layers, depth, width), gains, shifts)


def solution(mesh):
    placed = (
        P("dp", None, None, "chan"),
        P(None, None, None, "chan"),
        P(None, "chan"),
        P(None, "chan"),
    )
    return jax.shard_map(
        functools.partial(on_device, mesh.shape["dp"], mesh.shape["chan"]),
        mesh=mesh,
        in_specs=placed,
        out_specs=P("dp", None, None, "chan"),
        check_vma=False,
    )
```

```python
import functools

import jax
import jax.numpy as jnp
from jax import lax
from jax.experimental import pallas as pl
from jax.experimental.pallas import tpu as pltpu
from jax.sharding import PartitionSpec as P

EPSILON = 1e-05
MESH = pl.DeviceIdType.MESH
LANES = 128
VMEM_LIMIT = 57 * 1024 * 1024


def round_up(value, step):
    return -(-value // step) * step


def stack_kernel(
    ndp, nch, side, mine, layers, rows, base,
    boards, weights, gains, shifts, out,
    raw, board_send, board_other, wbuf, aff, xf, skip, mask, lhs, zbuf, near, stats, stage, stage_own,
    own_sem, a_local, x_send, x_recv, w_local, w_send, w_recv, n_send, n_recv, s_send, s_recv, o_send, o_recv,
):
    dp = lax.axis_index("dp")
    me = lax.axis_index("chan")
    other = 1 - me
    partner = (dp, other)
    total = ndp * nch
    stride = side + 1
    points = mine * side * side

    def flip(index, step):
        bit = 1
        while bit <= step:
            if step & bit:
                index = index + bit - 2 * bit * lax.rem(lax.div(index, bit), 2)
            bit *= 2
        return index

    def every_peer(body):
        if ndp <= 32 and ndp & (ndp - 1) == 0:
            for step in range(ndp - 1, 0, -1):
                body((flip(dp, step), me))
        else:
            def one(step, carry):
                body((lax.rem(dp + step, ndp), me))
                return carry
            lax.fori_loop(1, ndp, one, 0)

    barrier = pltpu.get_barrier_semaphore()
    every_peer(lambda peer: pl.semaphore_signal(barrier, inc=1, device_id=peer, device_id_type=MESH))

    pl.semaphore_signal(barrier, inc=1, device_id=partner, device_id_type=MESH)
    own = pltpu.make_async_copy(boards, raw, own_sem)
    own.start()
    affine_own = [
        pltpu.make_async_copy(gains, aff.at[me, 0], a_local.at[0]),
        pltpu.make_async_copy(shifts, aff.at[me, 1], a_local.at[1]),
    ]
    for one in affine_own:
        one.start()

    def weight_local(layer):
        return pltpu.make_async_copy(weights.at[layer], wbuf.at[me, layer], w_local.at[layer])

    def weight_remote(layer, half):
        return pltpu.make_async_remote_copy(
            src_ref=weights.at[layer], dst_ref=wbuf.at[half, layer],
            send_sem=w_send.at[layer], recv_sem=w_recv.at[layer],
            device_id=partner, device_id_type=MESH,
        )

    def swap(index, src, dst):
        return pltpu.make_async_remote_copy(
            src_ref=src, dst_ref=dst, send_sem=x_send.at[index], recv_sem=x_recv.at[index],
            device_id=partner, device_id_type=MESH,
        )

    for layer in range(layers):
        weight_local(layer).start()
    xf[...] = jnp.zeros_like(xf)
    mask[...] = jnp.zeros_like(mask)
    for n in range(mine):
        for i in range(side):
            mask[pl.ds((n * stride + i) * stride, side), :] = jnp.ones((side, LANES), jnp.float32)

    own.wait()
    for i in range(side):
        line = raw[i].astype(jnp.float32)
        for n in range(mine):
            at = base + (n * stride + i) * stride
            planes = [line[:, half * mine + n, :] for half in range(nch)]
            kept = jnp.where(me == 0, planes[0], planes[1])
            given = jnp.where(me == 0, planes[1], planes[0])
            xf[me, pl.ds(at, side), :] = kept
            board_send[n, i] = given.astype(jnp.bfloat16)

    pl.semaphore_wait(barrier, ndp)
    swaps = [
        swap(0, board_send, board_other),
        swap(1, gains, aff.at[me, 0]),
        swap(2, shifts, aff.at[me, 1]),
    ]
    swaps[0].start()
    weight_remote(0, me).start()
    swaps[1].start()
    swaps[2].start()

    def place(half, source):
        for n in range(mine):
            for i in range(side):
                at = base + (n * stride + i) * stride
                xf[half, pl.ds(at, side), :] = source[n, i].astype(jnp.float32)

    swaps[0].wait_recv()
    place(other, board_other)
    swaps[1].wait_recv()
    swaps[2].wait_recv()
    for one in affine_own:
        one.wait()

    def parity(layer):
        return layer % 2 if isinstance(layer, int) else lax.rem(layer, 2)

    def near_copy(layer):
        return pltpu.make_async_remote_copy(
            src_ref=near.at[layer, me], dst_ref=near.at[layer, me],
            send_sem=n_send.at[layer], recv_sem=n_recv.at[layer],
            device_id=partner, device_id_type=MESH,
        )

    def send_stats(layer):
        centre = (side // 2) * stride + side // 2
        for half in range(nch):
            lanes = pl.ds(half * LANES, LANES)
            middle = zbuf[pl.ds(centre, 1), lanes]
            away = (zbuf[:, lanes] - middle) * mask[...]
            first = jnp.sum(away, axis=0, keepdims=True)
            second = jnp.sum(away * away, axis=0, keepdims=True)
            near[layer, me, pl.ds(half, 1), :] = middle + first * (1.0 / points)
            near[layer, me, pl.ds(nch + half, 1), :] = second - first * first * (1.0 / points)

        near_copy(layer).start()
        near_copy(layer).wait_recv()
        pair = [near[layer, core] for core in range(nch)]
        drift = pair[1][:nch] - pair[0][:nch]
        stats[layer, dp, pl.ds(0, nch), :] = pair[0][:nch] + 0.5 * drift
        stats[layer, dp, pl.ds(nch, nch), :] = pair[0][nch:] + pair[1][nch:] + (0.5 * points) * drift * drift

        def send(peer):
            pltpu.make_async_remote_copy(
                src_ref=stats.at[layer, dp], dst_ref=stats.at[layer, dp],
                send_sem=s_send.at[layer], recv_sem=s_recv.at[layer],
                device_id=peer, device_id_type=MESH,
            ).start()

        every_peer(send)

        @pl.when(parity(layer) == 0)
        def _():
            for half in range(nch):
                skip[half] = xf[half, pl.ds(base, rows), :]

    def merged(layer):
        arrived = stats.at[layer, pl.ds(0, ndp - 1)]
        pltpu.make_async_copy(arrived, arrived, s_recv.at[layer]).wait()
        seen = stats[layer]
        mine_mean = stats[layer, dp, pl.ds(0, nch), :]
        drift = seen[:, :nch] - mine_mean[None]
        shifted = jnp.sum(drift, axis=0)
        spread = jnp.sum(points * nch * drift * drift + seen[:, nch:], axis=0)
        mean = mine_mean + shifted * (1.0 / ndp)
        var = (spread - shifted * shifted * (points * nch / ndp)) * (1.0 / (points * total))
        return mean, lax.rsqrt(var + EPSILON)

    def normalise(layer, half, mean, inverse):
        keep = 1.0 * parity(layer)
        gain = aff[half, 0, pl.ds(layer, 1), :] * inverse[half : half + 1]
        shift = aff[half, 1, pl.ds(layer, 1), :]
        normed = (zbuf[:, pl.ds(half * LANES, LANES)] - mean[half : half + 1]) * gain + shift
        normed = normed + skip[half] * keep
        fresh = jnp.maximum(normed, 0.0) * mask[...]
        xf[half, pl.ds(base, rows), :] = fresh.astype(jnp.bfloat16).astype(jnp.float32)

    def multiply(layer, half):
        for tap in range(9):
            a, b = divmod(tap, 3)
            at = base + (a - 1) * stride + (b - 1)
            lhs[half, :, pl.ds(tap * LANES, LANES)] = xf[half, pl.ds(at, rows), :].astype(jnp.bfloat16)
        kernel = jnp.concatenate([
            jnp.concatenate([
                wbuf[column, layer, pl.ds((tap * nch + half) * LANES, LANES), :] for column in range(nch)
            ], axis=1)
            for tap in range(9)
        ], axis=0)
        return jnp.dot(lhs[half], kernel, preferred_element_type=jnp.float32)

    def weights_ready(layer):
        weight_local(layer).wait()
        weight_remote(layer, other).wait_recv()

    if layers > 1:
        weight_remote(1, me).start()
    weights_ready(0)
    zbuf[...] = sum(multiply(0, half) for half in range(nch))
    send_stats(0)

    def layer_step(layer, carry):
        @pl.when(layer + 1 < layers)
        def _():
            weight_remote(layer + 1, me).start()

        weights_ready(layer)
        mean, inverse = merged(layer - 1)
        parts = []
        for half in range(nch):
            normalise(layer - 1, half, mean, inverse)
            parts.append(multiply(layer, half))
        zbuf[...] = sum(parts)
        send_stats(layer)
        return carry

    lax.fori_loop(1, layers, layer_step, 0)
    mean, inverse = merged(layers - 1)
    for half in range(nch):
        normalise(layers - 1, half, mean, inverse)

    def collect(half, target, first):
        for n in range(mine):
            for i in range(side):
                at = base + (n * stride + i) * stride
                target[first + n, i] = xf[half, pl.ds(at, side), :].astype(jnp.bfloat16)

    collect(other, stage, 0)
    final = pltpu.make_async_remote_copy(
        src_ref=stage, dst_ref=out.at[pl.ds(me * mine, mine)],
        send_sem=o_send, recv_sem=o_recv, device_id=partner, device_id_type=MESH,
    )
    final.start()
    collect(me, stage_own, 0)
    kept = pltpu.make_async_copy(stage_own, out.at[pl.ds(me * mine, mine)], own_sem)
    kept.start()

    for one in swaps:
        one.wait_send()

    def drain(layer, carry):
        weight_remote(layer, me).wait_send()
        near_copy(layer).wait_send()
        sent = stats.at[layer, pl.ds(0, ndp - 1)]
        pltpu.make_async_copy(sent, sent, s_send.at[layer]).wait()
        return carry

    lax.fori_loop(0, layers, drain, 0)
    kept.wait()
    final.wait()


def on_device(ndp, nch, boards, weights, gains, shifts):
    held, side, _, width = boards.shape
    layers = weights.shape[0]
    mine = held // nch
    stride = side + 1
    rows = round_up((mine - 1) * stride * stride + side * stride, 16)
    base = round_up(stride + 1, 8)
    span = round_up(base + rows + stride + 1, 8)
    total = ndp * nch
    depth = 9 * width * nch
    dma = pltpu.SemaphoreType.DMA
    in_hbm = pl.BlockSpec(memory_space=pltpu.HBM)
    return pl.pallas_call(
        functools.partial(stack_kernel, ndp, nch, side, mine, layers, rows, base),
        out_shape=jax.ShapeDtypeStruct(boards.shape, jnp.bfloat16),
        in_specs=[in_hbm] * 4,
        out_specs=in_hbm,
        scratch_shapes=[
            pltpu.VMEM((side, side, held, width), jnp.bfloat16),
            pltpu.VMEM((mine, side, side, width), jnp.bfloat16),
            pltpu.VMEM((mine, side, side, width), jnp.bfloat16),
            pltpu.VMEM((nch, layers, depth, width), jnp.bfloat16),
            pltpu.VMEM((nch, 2, layers, width), jnp.float32),
            pltpu.VMEM((nch, span, width), jnp.float32),
            pltpu.VMEM((nch, rows, width), jnp.float32),
            pltpu.VMEM((rows, width), jnp.float32),
            pltpu.VMEM((nch, rows, depth // nch), jnp.bfloat16),
            pltpu.VMEM((rows, width * nch), jnp.float32),
            pltpu.VMEM((layers, nch, 2 * nch, width), jnp.float32),
            pltpu.VMEM((layers, ndp, 2 * nch, width), jnp.float32),
            pltpu.VMEM((mine, side, side, width), jnp.bfloat16),
            pltpu.VMEM((mine, side, side, width), jnp.bfloat16),
            dma, dma((2,)), dma((3,)), dma((3,)),
            dma((layers,)), dma((layers,)), dma((layers,)),
            dma((layers,)), dma((layers,)), dma((layers,)), dma((layers,)), dma, dma,
        ],
        compiler_params=pltpu.CompilerParams(
            collective_id=0, has_side_effects=True, vmem_limit_bytes=VMEM_LIMIT
        ),
        cost_estimate=pl.CostEstimate(
            flops=2 * layers * rows * depth * width * nch,
            bytes_accessed=2 * weights.size + 4 * boards.size,
            transcendentals=0,
        ),
    )(boards.transpose(1, 2, 0, 3), weights.reshape(layers, depth, width), gains, shifts)


def solution(mesh):
    placed = (
        P("dp", None, None, "chan"),
        P(None, None, None, "chan"),
        P(None, "chan"),
        P(None, "chan"),
    )
    return jax.shard_map(
        functools.partial(on_device, mesh.shape["dp"], mesh.shape["chan"]),
        mesh=mesh,
        in_specs=placed,
        out_specs=P("dp", None, None, "chan"),
        check_vma=False,
    )
```
